32 devices in a mesh: dp: 8 (over y, x, core), region: 4 (over z).
Axes of the slice: x: 2, y: 2, z: 4, core: 2. Of those that a mesh axis runs over, the one named last changes fastest.
Arguments:
- inputs: bfloat16 [8, 2, 1024, 256], P('dp', None, 'region'), may hold values from -6 to 6
- cotangent: bfloat16 [8, 2, 1024, 256], P('dp', None, 'region'), may hold values from -6 to 6
- w_filter: bfloat16 [2, 256, 256], replicated, may hold values from -0.25 to 0.25
- w_gate: bfloat16 [2, 256, 256], replicated, may hold values from -0.25 to 0.25
- w_mix: bfloat16 [2, 256, 256], replicated, may hold values from -0.25 to 0.25
- neighbours: int32 [8, 6], replicated, may hold values from 0 to 7, as said below
- adjacency: bfloat16 [8, 6, 128, 128], P('region'), may hold values from -0.21875 to 0.21875
Outputs:
- grad_inputs: bfloat16 [8, 2, 1024, 256], P('dp', None, 'region')
- grad_filter: float32 [2, 256, 256], replicated
- grad_gate: float32 [2, 256, 256], replicated
- grad_mix: float32 [2, 256, 256], replicated
The draws below stay inside these ranges and needn't reach their ends.
Inputs may be any that keep to these rules, and one draw needn't show every extreme that they name: `neighbours`: for every region r (tiles r * 2 to (r + 1) * 2 - 1), exactly 3 of the 12 entries of its tiles' lists name tiles of other regions, each of a different region, so at most 1 name tiles of any one other region; all other entries name tiles of region r.
All inputs are finite; a program needn't handle non-finite values.
Results may differ from the reference program's by a relative error of at most 0.0053.
Values may be sent and summed in bfloat16 or wider, within the bound.
No kernel may reach another device: no remote copies, remote signals or barrier semaphores. Data moves between devices by JAX's collectives and lax.ppermute only.
A program may use at most 64 MiB of HBM per device.

```python
import math
import jax
import jax.numpy as jnp
from jax import lax

C = 256
TILE = 128
NB = 6
TL = 2
TILES_DEV = 2
TILES = 8
SITES = 1024
BATCH = 8


def draw_neighbours(key, part):
    regions = TILES // TILES_DEV
    entries = TILES_DEV * NB
    foreign = min(entries - 1, regions - 1)

    def one_region(region, region_key):
        other_key, entry_key, local_key = jax.random.split(region_key, 3)
        offsets = jnp.arange(1, regions, dtype=jnp.int32)
        spread = jax.random.permutation(other_key, regions - 1).astype(jnp.int32)
        scores = jnp.where(offsets == 1, 0, jnp.where(offsets == regions - 1, 1, jnp.where(offsets == regions // 2, 2, 3 + spread)))
        order_keys = jnp.argsort(scores, stable=True)
        chosen = offsets[order_keys][:foreign]
        others = (region + chosen) % regions
        owner_list = jnp.concatenate([others.astype(jnp.int32), jnp.full((entries - foreign,), region, jnp.int32)])
        order = jax.random.permutation(entry_key, entries)
        owners = owner_list[order]
        local_tile = jax.random.randint(local_key, (entries,), 0, TILES_DEV)
        return (owners * TILES_DEV + local_tile).astype(jnp.int32)
    region_keys = jax.random.split(jax.random.fold_in(key, 17), regions)
    table = jax.vmap(one_region)(jnp.arange(regions, dtype=jnp.int32), region_keys)
    return table.reshape(TILES, NB)


def shard_levels(stream_key, dims, cuts, least, top_value):
    level, own = 1.0, jax.random.fold_in(stream_key, 6)
    for axis_at, blocks in cuts:
        draws = jnp.exp(jax.random.uniform(jax.random.fold_in(own, axis_at), (blocks,), jnp.float32, least / len(cuts), top_value / len(cuts)))
        level = level * jnp.repeat(draws, dims[axis_at] // blocks).reshape([-1 if axis == axis_at else 1 for axis in range(len(dims))])
    return level


def bell_draw(rng, shape, deviation, limit, cuts=(), held_as=jnp.bfloat16):
    factor_of = shard_levels(rng, shape, cuts, -0.22, 0.18) if cuts else 1.0
    array = jax.random.normal(rng, shape, jnp.float32) * deviation * factor_of
    return jnp.minimum(jnp.maximum(array, -limit), limit).astype(held_as)


def setup_inputs(seed: int = 0) -> dict:
    splits = jax.random.split(jax.random.key(seed), 8)
    inputs = bell_draw(splits[0], (BATCH, TL, SITES, C), 1.0, 6.0, ((0, 8), (2, 4)))
    cotangent = bell_draw(splits[1], (BATCH, TL, SITES, C), 1.0, 6.0, ((0, 8), (2, 4)))
    w_filter = bell_draw(splits[2], (2, C, C), (2 * C) ** -0.5, 0.25)
    w_gate = bell_draw(splits[3], (2, C, C), (2 * C) ** -0.5, 0.25)
    w_mix = bell_draw(splits[4], (2, C, C), (2 * C) ** -0.5, 0.25)
    neighbours = draw_neighbours(jax.random.fold_in(splits[7], 71), 0)
    adjacency = bell_draw(splits[6], (TILES, NB, TILE, TILE), (NB * TILE) ** -0.5, 0.21875, ((0, 4),))
    return dict(inputs=inputs, cotangent=cotangent, w_filter=w_filter, w_gate=w_gate, w_mix=w_mix, neighbours=neighbours, adjacency=adjacency)


def reference(inputs, cotangent, w_filter, w_gate, w_mix, neighbours, adjacency):
    w_cat = jnp.concatenate([jnp.concatenate([w_filter[0], w_gate[0]], axis=1), jnp.concatenate([w_filter[1], w_gate[1]], axis=1)], axis=0)
    w_mixed = w_mix.reshape(2 * C, C)
    adj_wide = adjacency.astype(jnp.float32)
    flat_ids = neighbours.reshape(-1).astype(jnp.int32)

    def one_window(carry, pair):
        conv_sum, mix_sum = carry
        window_in, window_cot = pair
        previous = jnp.concatenate([jnp.zeros_like(window_in[:1]), window_in[:-1]], axis=0)
        joint = jnp.concatenate([window_in, previous], axis=-1).reshape(-1, 2 * C)
        act = jnp.dot(joint, w_cat, preferred_element_type=jnp.float32)
        filt = jnp.tanh(act[:, :C])
        gate = jax.nn.sigmoid(act[:, C:])
        hidden = (filt * gate).astype(jnp.bfloat16)
        tiled = hidden.reshape(TL, TILES, TILE, C)
        picked = tiled[:, neighbours].astype(jnp.float32)
        graph = jnp.einsum('jkpq,tjkqc->tjpc', adj_wide, picked).astype(jnp.bfloat16)
        both = jnp.concatenate([hidden, graph.reshape(-1, C)], axis=-1)
        cot_rows = window_cot.reshape(-1, C)
        mix_sum = mix_sum + jnp.dot(both.T, cot_rows, preferred_element_type=jnp.float32)
        back = jnp.dot(cot_rows, w_mixed.T, preferred_element_type=jnp.float32)
        direct = back[:, :C]
        graph_cot = back[:, C:].astype(jnp.bfloat16).reshape(TL, TILES, TILE, C)
        term = jnp.einsum('jkpq,tjpc->tjkqc', adj_wide, graph_cot.astype(jnp.float32)).astype(jnp.bfloat16)
        term_rows = jnp.transpose(term, (1, 2, 0, 3, 4)).reshape(TILES * NB, TL, TILE, C).astype(jnp.float32)
        summed = jax.ops.segment_sum(term_rows, flat_ids, num_segments=TILES)
        grad_hidden = direct + jnp.transpose(summed, (1, 0, 2, 3)).reshape(-1, C)
        act_cot = jnp.concatenate([grad_hidden * gate * (1.0 - filt * filt), grad_hidden * filt * gate * (1.0 - gate)], axis=-1).astype(jnp.bfloat16)
        conv_sum = conv_sum + jnp.dot(joint.T, act_cot, preferred_element_type=jnp.float32)
        back_in = jnp.dot(act_cot, w_cat.T, preferred_element_type=jnp.float32).reshape(TL, SITES, 2 * C)
        later = jnp.concatenate([back_in[1:, :, C:], jnp.zeros((1, SITES, C), jnp.float32)], axis=0)
        grad_in = (window_cot.astype(jnp.float32) + back_in[:, :, :C] + later).astype(jnp.bfloat16)
        return ((conv_sum, mix_sum), grad_in)
    start = (jnp.zeros((2 * C, 2 * C), jnp.float32), jnp.zeros((2 * C, C), jnp.float32))
    (conv_sum, mix_sum), grad_inputs = lax.scan(one_window, start, (inputs, cotangent))
    factor = 1.0 / math.sqrt(BATCH * TL * SITES)
    grad_filter = (conv_sum[:, :C] * factor).reshape(2, C, C)
    grad_gate = (conv_sum[:, C:] * factor).reshape(2, C, C)
    grad_mix = (mix_sum * factor).reshape(2, C, C)
    return (grad_inputs, grad_filter, grad_gate, grad_mix)
```

```python
import functools
import math

import jax
import jax.numpy as jnp
from jax import lax
from jax.experimental import pallas as pl
from jax.experimental.pallas import tpu as pltpu
from jax.sharding import PartitionSpec as P

TILE = 128
F32 = jnp.float32
BF16 = jnp.bfloat16
VM = pl.BlockSpec(memory_space=pltpu.VMEM)
SM = pl.BlockSpec(memory_space=pltpu.SMEM)


def dot(a, b, ca, cb):
    return lax.dot_general(a, b, (((ca,), (cb,)), ((), ())), preferred_element_type=F32)


def call(body, outs, n_smem, n_vmem, scratch=(), flops=0, nbytes=0, name=None):
    return pl.pallas_call(
        body,
        out_shape=outs,
        in_specs=[SM] * n_smem + [VM] * n_vmem,
        out_specs=[VM] * len(outs),
        scratch_shapes=list(scratch),
        cost_estimate=pl.CostEstimate(flops=flops, bytes_accessed=nbytes, transcendentals=0),
        compiler_params=pltpu.CompilerParams(vmem_limit_bytes=40 * 1024 * 1024),
        name=name,
    )


def find_entry(nb_ref, source, target, tiles, per_tile):
    tile = jnp.int32(0)
    place = jnp.int32(0)
    named = jnp.int32(-1)
    for j in range(tiles):
        for k in range(per_tile):
            local = nb_ref[source * tiles + j, k] - target * tiles
            hit = jnp.logical_and(local >= 0, local < tiles)
            tile = jnp.where(hit, j, tile)
            place = jnp.where(hit, k, place)
            named = jnp.where(hit, local, named)
    return tile, place, named


def outgoing_body(regions, ids_ref, nb_ref, cot_ref, adj_ref, *out_refs):
    me = ids_ref[0]
    tiles, per_tile = adj_ref.shape[:2]
    for s in range(1, regions):
        other = lax.rem(me + s, regions)
        tile, place, named = find_entry(nb_ref, me, other, tiles, per_tile)
        out = out_refs[s - 1]

        @pl.when(named >= 0)
        def _():
            weights = adj_ref[tile, place]
            for t in range(cot_ref.shape[0]):
                rows = cot_ref[t, pl.ds(pl.multiple_of(tile * TILE, TILE), TILE), :]
                out[t] = dot(weights, rows, 0, 0).astype(BF16)

        @pl.when(named < 0)
        def _():
            out[...] = jnp.zeros_like(out)


def local_body(
    steps, ids_ref, nb_ref, x_ref, cot_ref, wf_ref, wg_ref, wm_ref, adj_ref,
    hidden_ref, df_ref, dg_ref, direct_ref, local_ref, mix_ref,
):
    me = ids_ref[0]
    tiles, per_tile = adj_ref.shape[:2]
    total = cot_ref.shape[0]
    mix = jnp.zeros(mix_ref.shape, F32)
    for t in range(total):
        x = x_ref[t]
        act_f = dot(x, wf_ref[0], 1, 0)
        act_g = dot(x, wg_ref[0], 1, 0)
        if t % steps:
            before = x_ref[t - 1]
            act_f += dot(before, wf_ref[1], 1, 0)
            act_g += dot(before, wg_ref[1], 1, 0)
        filt = jnp.tanh(act_f)
        gate = jax.nn.sigmoid(act_g)
        both = filt * gate
        hidden = both.astype(BF16)
        hidden_ref[t] = hidden
        df_ref[t] = gate * (1.0 - filt * filt)
        dg_ref[t] = both * (1.0 - gate)
        cot = cot_ref[t]
        direct_ref[t] = dot(cot, wm_ref[0], 1, 1)
        mix += dot(hidden, cot, 0, 0)
    mix_ref[...] = mix
    local_ref[...] = jnp.zeros_like(local_ref)
    for j in range(tiles):
        for k in range(per_tile):
            local = nb_ref[me * tiles + j, k] - me * tiles

            @pl.when(jnp.logical_and(local >= 0, local < tiles))
            def _():
                place = pl.ds(pl.multiple_of(local * TILE, TILE), TILE)
                for t in range(total):
                    local_ref[t, place, :] += dot(adj_ref[j, k], cot_ref[t, j * TILE : (j + 1) * TILE, :], 0, 0)


def gradient_body(
    regions, steps, per_tile, ids_ref, nb_ref, x_ref, hidden_ref, df_ref, dg_ref, direct_ref, local_ref, mix_ref, wm_ref, *refs
):
    arrived, (act_ref, keep_ref, send_ref), (sums, parts) = refs[: regions - 1], refs[regions - 1 : -2], refs[-2:]
    me, core = ids_ref[0], ids_ref[1]
    total, sites, chans = x_ref.shape
    tiles = sites // TILE
    sums[...] = local_ref[...]
    for s in range(1, regions):
        source = lax.rem(me - s + regions, regions)
        _, _, named = find_entry(nb_ref, source, me, tiles, per_tile)

        @pl.when(named >= 0)
        def _():
            place = pl.ds(pl.multiple_of(named * TILE, TILE), TILE)
            for t in range(total):
                sums[t, place, :] += arrived[s - 1][t].astype(F32)

    zero = jnp.zeros((chans, chans), F32)
    conv = [[zero, zero], [zero, zero]]
    mix = zero
    for t in range(total):
        summed = sums[t].astype(BF16)
        mix += dot(hidden_ref[t], summed, 0, 0)
        grad = direct_ref[t] + dot(summed, wm_ref[1], 1, 1)
        for part, factor in enumerate((df_ref, dg_ref)):
            act = (grad * factor[t]).astype(BF16)
            act_ref[part, t] = act
            conv[part][0] += dot(x_ref[t], act, 0, 0)
            if t % steps:
                conv[part][1] += dot(x_ref[t - 1], act, 0, 0)
    for tap in range(2):
        parts[tap, 0] = conv[0][tap]
        parts[tap, 1] = conv[1][tap]
    parts[0, 2] = mix_ref[...]
    parts[1, 2] = mix
    keep_ref[...] = parts[core]
    send_ref[...] = parts[1 - core].astype(BF16)


def inputs_body(steps, cot_ref, act_ref, wf_ref, wg_ref, out_ref):
    total = cot_ref.shape[0]
    for t in range(total):
        grad = cot_ref[t].astype(F32)
        grad += dot(act_ref[0, t], wf_ref[0], 1, 1) + dot(act_ref[1, t], wg_ref[0], 1, 1)
        if (t + 1) % steps:
            grad += dot(act_ref[0, t + 1], wf_ref[1], 1, 1) + dot(act_ref[1, t + 1], wg_ref[1], 1, 1)
        out_ref[t] = grad.astype(BF16)


def split_body(chips, ids_ref, keep_ref, got_ref, own_ref, *rest):
    sends, both = rest[:-1], rest[-1]
    chip = ids_ref[2]
    rows = own_ref.shape[1]
    both[...] = keep_ref[...] + got_ref[...].astype(F32)
    own_ref[...] = both[:, pl.ds(pl.multiple_of(chip * rows, rows), rows), :]
    for p in range(1, chips):
        other = partner(chip, p, chips)
        sends[p - 1][...] = both[:, pl.ds(pl.multiple_of(other * rows, rows), rows), :].astype(BF16)


def add_body(own_ref, *refs):
    total = own_ref[...]
    for got in refs[:-1]:
        total += got[...].astype(F32)
    refs[-1][...] = total.astype(BF16)


def region_sum_body(regions, ids_ref, own_ref, *refs):
    gots, out_ref, slots = refs[: regions - 1], refs[-2], refs[-1]
    me = ids_ref[0]
    slots[me] = own_ref[...]
    for s in range(1, regions):
        slots[lax.rem(me - s + regions, regions)] = gots[s - 1][...]
    total = slots[0].astype(F32)
    for r in range(1, regions):
        total += slots[r].astype(F32)
    out_ref[...] = total.astype(BF16)


def scale_body(chips, factor, ids_ref, *refs):
    chunks, outs = refs[: 2 * chips], refs[2 * chips :]
    core, chip = ids_ref[1], ids_ref[2]
    rows = chunks[0].shape[1]
    for c in range(2):
        tap = core if c == 0 else 1 - core
        for p in range(chips):
            other = partner(chip, p, chips)
            place = pl.ds(pl.multiple_of(other * rows, rows), rows)
            for a in range(3):
                outs[a][tap, place, :] = chunks[c * chips + p][a].astype(F32) * factor


def partner(chip, p, chips):
    return jnp.bitwise_xor(chip, p)


def chip_pairs(chips, p):
    return [(2 * c + b, 2 * (c ^ p) + b) for c in range(chips) for b in range(2)]


def per_device(inputs, cotangent, w_filter, w_gate, w_mix, neighbours, adjacency):
    regions = lax.axis_size("region")
    dp = lax.axis_size("dp")
    chips = dp // 2
    region = lax.axis_index("region").astype(jnp.int32)
    place = lax.axis_index("dp").astype(jnp.int32)
    ids = jnp.stack([region, place % 2, place // 2])
    windows, steps, sites, chans = inputs.shape
    total = windows * steps
    per_tile = neighbours.shape[1]
    x = inputs.reshape(total, sites, chans)
    cot = cotangent.reshape(total, sites, chans)
    shape = jax.ShapeDtypeStruct
    block = total * sites * chans

    outgoing = call(
        functools.partial(outgoing_body, regions),
        [shape((total, TILE, chans), BF16)] * (regions - 1), 2, 2, name="outgoing",
        flops=2 * (regions - 1) * total * TILE * TILE * chans, nbytes=4 * block,
    )(ids, neighbours, cot, adjacency)
    arrived = [
        lax.ppermute(part, "region", [(r, (r + s) % regions) for r in range(regions)])
        for s, part in enumerate(outgoing, 1)
    ]
    hidden, d_filter, d_gate, direct, local, mix = call(
        functools.partial(local_body, steps),
        [shape(x.shape, BF16)] + [shape(x.shape, F32)] * 4 + [shape((chans, chans), F32)], 2, 6, name="local",
        flops=14 * block * chans, nbytes=30 * block,
    )(ids, neighbours, x, cot, w_filter, w_gate, w_mix, adjacency)
    act_cot, keep, send = call(
        functools.partial(gradient_body, regions, steps, per_tile),
        [shape((2,) + x.shape, BF16), shape((3, chans, chans), F32), shape((3, chans, chans), BF16)],
        2, 8 + regions - 1, name="gradient",
        scratch=[pltpu.VMEM(x.shape, F32), pltpu.VMEM((2, 3, chans, chans), F32)],
        flops=10 * block * chans, nbytes=30 * block,
    )(ids, neighbours, x, hidden, d_filter, d_gate, direct, local, mix, w_mix, *arrived)
    (grad_inputs,) = call(
        functools.partial(inputs_body, steps), [shape(x.shape, BF16)], 0, 4, name="inputs",
        flops=8 * block * chans, nbytes=16 * block,
    )(cot, act_cot, w_filter, w_gate)

    rows = chans // chips
    chunk = (3, rows, chans)
    got = lax.ppermute(send, "dp", [(i, i ^ 1) for i in range(dp)])
    own, *sends = call(
        functools.partial(split_body, chips), [shape(chunk, F32)] + [shape(chunk, BF16)] * (chips - 1), 1, 2,
        scratch=[pltpu.VMEM((3, chans, chans), F32)], name="split",
    )(ids, keep, got)
    gots = [lax.ppermute(part, "dp", chip_pairs(chips, p)) for p, part in enumerate(sends, 1)]
    (mine,) = call(add_body, [shape(chunk, BF16)], 0, chips, name="add")(own, *gots)
    gots = [lax.ppermute(mine, "region", [(r, (r + s) % regions) for r in range(regions)]) for s in range(1, regions)]
    (done,) = call(
        functools.partial(region_sum_body, regions), [shape(chunk, BF16)], 1, regions,
        scratch=[pltpu.VMEM((regions,) + chunk, BF16)], name="region_sum",
    )(ids, mine, *gots)
    chunks = [done] + [lax.ppermute(done, "dp", chip_pairs(chips, p)) for p in range(1, chips)]
    chunks += [lax.ppermute(part, "dp", [(i, i ^ 1) for i in range(dp)]) for part in chunks]
    factor = 1.0 / math.sqrt(windows * dp * steps * sites * regions)
    grads = call(
        functools.partial(scale_body, chips, factor), [shape((2, chans, chans), F32)] * 3, 1, 2 * chips, name="scale"
    )(ids, *chunks)
    return (grad_inputs.reshape(inputs.shape), *grads)


def solution(mesh):
    return jax.shard_map(
        per_device,
        mesh=mesh,
        in_specs=(
            P("dp", None, "region", None),
            P("dp", None, "region", None),
            P(),
            P(),
            P(),
            P(),
            P("region", None, None, None),
        ),
        out_specs=(P("dp", None, "region", None), P(), P(), P()),
        check_vma=False,
    )
```

```python
import functools
import math

import jax
import jax.numpy as jnp
from jax import lax
from jax.experimental import pallas as pl
from jax.experimental.pallas import tpu as pltpu
from jax.sharding import PartitionSpec as P

TILE = 128
F32 = jnp.float32
BF16 = jnp.bfloat16
VM = pl.BlockSpec(memory_space=pltpu.VMEM)
HB = pl.BlockSpec(memory_space=pltpu.HBM)
BOTH = ("dp", "region")


def dot(a, b, ca=1, cb=0):
    return lax.dot_general(a, b, (((ca,), (cb,)), ((), ())), preferred_element_type=F32)


def call(body, outs, ins, name, out_specs=None, scratch=(), flops=0, nbytes=0, aliases=None):
    return pl.pallas_call(
        body,
        out_shape=outs,
        in_specs=ins,
        out_specs=out_specs or [VM] * len(outs),
        scratch_shapes=list(scratch),
        cost_estimate=pl.CostEstimate(flops=flops, bytes_accessed=nbytes, transcendentals=0),
        compiler_params=pltpu.CompilerParams(vmem_limit_bytes=40 * 1024 * 1024),
        input_output_aliases=aliases or {},
        name=name,
    )


def fetch(pairs, sems):
    copies = [pltpu.make_async_copy(src, dst, sems.at[i]) for i, (src, dst) in enumerate(pairs)]
    for copy in copies:
        copy.start()
    return copies


def find_entry(nb_ref, source, target, tiles, per_tile):
    tile = jnp.int32(0)
    place = jnp.int32(0)
    named = jnp.int32(-1)
    for j in range(tiles):
        for k in range(per_tile):
            local = nb_ref[source * tiles + j, k] - target * tiles
            hit = jnp.logical_and(local >= 0, local < tiles)
            tile = jnp.where(hit, j, tile)
            place = jnp.where(hit, k, place)
            named = jnp.where(hit, local, named)
    return tile, place, named


def region_of():
    return lax.axis_index("region").astype(jnp.int32)


def lane_of():
    place = lax.axis_index("dp").astype(jnp.int32)
    lane, chip, region = jnp.bitwise_and(place, 1), lax.shift_right_logical(place, 1), region_of()
    return lane, jnp.where(lane == 0, chip, region), jnp.where(lane == 0, region, chip)


def outgoing_body(regions, order, nb_hbm, cot_hbm, adj_hbm, *refs):
    out_refs, (nb_ref, cot_ref, adj_ref, sems) = refs[: regions - 1], refs[regions - 1 :]
    me = region_of()
    tiles, per_tile = adj_ref.shape[:2]
    total = cot_ref.shape[0]
    first, *copies = fetch(
        [(nb_hbm, nb_ref)]
        + [(cot_hbm.at[t], cot_ref.at[t]) for t in range(total)]
        + [(adj_hbm.at[j], adj_ref.at[j]) for j in range(tiles)],
        sems,
    )
    first.wait()
    found = [find_entry(nb_ref, me, jnp.bitwise_xor(me, p), tiles, per_tile) for p in order]
    for copy in copies:
        copy.wait()
    for out, (tile, place, named) in zip(out_refs, found):

        @pl.when(named >= 0)
        def _():
            weights = adj_ref[tile, place]
            for t in range(total):
                rows = cot_ref[t, pl.ds(pl.multiple_of(tile * TILE, TILE), TILE), :]
                out[t] = dot(weights, rows, 0, 0).astype(BF16)

        @pl.when(named < 0)
        def _():
            out[...] = jnp.zeros_like(out)


def local_body(
    steps, order, nb_hbm, x_hbm, cot_hbm, wf_hbm, wg_hbm, wm_hbm, adj_hbm,
    df_ref, dg_ref, direct_ref, local_ref, mix_ref, xt_ref, ht_ref, wt_ref, mask_ref,
    nb_ref, x_ref, cot_ref, wf_ref, wg_ref, wm_ref, adj_ref, sems,
):
    me = region_of()
    tiles, per_tile = adj_ref.shape[:2]
    total = cot_ref.shape[0]
    c_nb, c_x, c_wf, c_wg, c_cot, c_wm, c_adj = fetch(
        [(nb_hbm, nb_ref), (x_hbm, x_ref), (wf_hbm, wf_ref), (wg_hbm, wg_ref), (cot_hbm, cot_ref), (wm_hbm, wm_ref), (adj_hbm, adj_ref)],
        sems,
    )
    c_x.wait()
    c_wf.wait()
    c_wg.wait()
    for t in range(total):
        x = x_ref[t]
        act_f = dot(x, wf_ref[0])
        act_g = dot(x, wg_ref[0])
        if t % steps:
            before = x_ref[t - 1]
            act_f += dot(before, wf_ref[1])
            act_g += dot(before, wg_ref[1])
        filt = jnp.tanh(act_f)
        gate = jax.nn.sigmoid(act_g)
        both = filt * gate
        ht_ref[t] = both.astype(BF16).T
        xt_ref[t] = x.T
        df_ref[t] = gate * (1.0 - filt * filt)
        dg_ref[t] = both * (1.0 - gate)
    c_cot.wait()
    c_wm.wait()
    wt_ref[...] = wm_ref[1].T
    mix = jnp.zeros(mix_ref.shape, F32)
    for t in range(total):
        cot = cot_ref[t]
        direct_ref[t] = dot(cot, wm_ref[0], 1, 1)
        mix += dot(ht_ref[t], cot)
    mix_ref[...] = mix
    local_ref[...] = jnp.zeros_like(local_ref)
    c_nb.wait()
    c_adj.wait()
    for j in range(tiles):
        for k in range(per_tile):
            local = nb_ref[me * tiles + j, k] - me * tiles

            @pl.when(jnp.logical_and(local >= 0, local < tiles))
            def _():
                place = pl.ds(pl.multiple_of(local * TILE, TILE), TILE)
                for t in range(total):
                    local_ref[t, place, :] += dot(adj_ref[j, k], cot_ref[t, j * TILE : (j + 1) * TILE, :], 0, 0)

    for s, p in enumerate(order):
        _, _, named = find_entry(nb_ref, jnp.bitwise_xor(me, p), me, tiles, per_tile)
        for j in range(tiles):
            mask_ref[s, j] = jnp.full(mask_ref.shape[2:], jnp.where(named == j, 1.0, 0.0), F32)


def tap_rows(tap, part, steps, xt_ref, act_ref):
    total = xt_ref.shape[0]
    if tap == 0:
        terms = [dot(xt_ref[t], act_ref[part, t]) for t in range(total)]
    else:
        terms = [dot(xt_ref[t - 1], act_ref[part, t]) for t in range(total) if t % steps]
    return functools.reduce(jnp.add, terms)


def half_of(tap, steps, xt_ref, ht_ref, mix_ref, act_ref, sums_ref):
    if tap == 0:
        mix = mix_ref[...]
    else:
        mix = functools.reduce(jnp.add, [dot(ht_ref[t], sums_ref[t]) for t in range(ht_ref.shape[0])])
    return [tap_rows(tap, 0, steps, xt_ref, act_ref), tap_rows(tap, 1, steps, xt_ref, act_ref), mix]


def send_body(regions, steps, df_ref, dg_ref, direct_ref, local_ref, mix_ref, xt_ref, ht_ref, wt_ref, mask_ref, *refs):
    arrived, (act_ref, sums_ref, send_ref) = refs[: regions - 1], refs[regions - 1 :]
    lane, _, _ = lane_of()
    total, sites, _ = local_ref.shape
    tiles = sites // TILE
    for t in range(total):
        summed = []
        for j in range(tiles):
            part = local_ref[t, j * TILE : (j + 1) * TILE, :]
            for s in range(regions - 1):
                part += mask_ref[s, j, :1] * arrived[s][t].astype(F32)
            summed.append(part.astype(BF16))
        summed = jnp.concatenate(summed, axis=0)
        sums_ref[t] = summed
        grad = direct_ref[t] + dot(summed, wt_ref[...])
        act_ref[0, t] = (grad * df_ref[t]).astype(BF16)
        act_ref[1, t] = (grad * dg_ref[t]).astype(BF16)
    for tap in range(2):

        @pl.when(lane == 1 - tap)
        def _():
            for i, part in enumerate(half_of(tap, steps, xt_ref, ht_ref, mix_ref, act_ref, sums_ref)):
                send_ref[i] = part.astype(BF16)


def keep_body(steps, mix_ref, xt_ref, ht_ref, act_ref, sums_ref, cot_ref, wf_ref, wg_ref, keep_ref, out_ref):
    lane, _, _ = lane_of()
    for tap in range(2):

        @pl.when(lane == tap)
        def _():
            for i, part in enumerate(half_of(tap, steps, xt_ref, ht_ref, mix_ref, act_ref, sums_ref)):
                keep_ref[i] = part

    total = cot_ref.shape[0]
    for t in range(total):
        grad = cot_ref[t].astype(F32)
        grad += dot(act_ref[0, t], wf_ref[0], 1, 1) + dot(act_ref[1, t], wg_ref[0], 1, 1)
        if (t + 1) % steps:
            grad += dot(act_ref[0, t + 1], wf_ref[1], 1, 1) + dot(act_ref[1, t + 1], wg_ref[1], 1, 1)
        out_ref[t] = grad.astype(BF16)


def split_body(ways, keep_ref, got_ref, own_ref, *sends):
    _, mine, _ = lane_of()
    rows = own_ref.shape[1]

    def chunk(p):
        place = pl.ds(pl.multiple_of(jnp.bitwise_xor(mine, p) * rows, rows), rows)
        return keep_ref[:, place, :] + got_ref[:, place, :].astype(F32)

    own_ref[...] = chunk(0)
    for p, send in enumerate(sends, 1):
        send[...] = chunk(p).astype(BF16)


def tree(parts):
    while len(parts) > 1:
        parts = [parts[i] + parts[i + 1] for i in range(0, len(parts), 2)]
    return parts[0]


def add_body(*refs):
    refs[-1][...] = tree([ref[...].astype(F32) for ref in refs[:-1]]).astype(BF16)


def scale_body(ways, factor, other, *refs):
    chunks, refs = refs[:ways], refs[ways:]
    outs, (held, sems) = refs[-5:-2], refs[-2:]
    lane, first, second = lane_of()
    tap, mine = (1 - lane, second) if other else (lane, first)
    rows = chunks[0].shape[1]
    copies = []
    for p in range(ways):
        place = pl.ds(pl.multiple_of(jnp.bitwise_xor(mine, p) * rows, rows), rows)
        for a in range(3):
            held[p, a] = chunks[p][a].astype(F32) * factor
            copy = pltpu.make_async_copy(held.at[p, a], outs[a].at[tap, place], sems.at[p, a])
            copy.start()
            copies.append(copy)
    for copy in copies:
        copy.wait()


def per_device(inputs, cotangent, w_filter, w_gate, w_mix, neighbours, adjacency):
    regions = lax.axis_size("region")
    dp = lax.axis_size("dp")
    ways = dp // 2
    assert ways == regions
    windows, steps, sites, chans = inputs.shape
    total = windows * steps
    tiles, per_tile = adjacency.shape[:2]
    x = inputs.reshape(total, sites, chans)
    cot = cotangent.reshape(total, sites, chans)
    shape = jax.ShapeDtypeStruct
    block = total * sites * chans
    order = sorted(range(1, regions), key=lambda p: p < regions // 2)
    dma = pltpu.SemaphoreType.DMA

    outgoing = call(
        functools.partial(outgoing_body, regions, order),
        [shape((total, TILE, chans), BF16)] * (regions - 1), [HB] * 3, "outgoing",
        scratch=[
            pltpu.SMEM(neighbours.shape, jnp.int32), pltpu.VMEM(cot.shape, BF16), pltpu.VMEM(adjacency.shape, BF16),
            dma((1 + total + tiles,)),
        ],
        flops=2 * (regions - 1) * total * TILE * TILE * chans, nbytes=4 * block,
    )(neighbours, cot, adjacency)
    arrived = [
        lax.ppermute(part, "region", [(r, r ^ p) for r in range(regions)]) for p, part in zip(order, outgoing)
    ]
    square = shape((chans, chans), F32)
    turned = shape((total, chans, sites), BF16)
    d_filter, d_gate, direct, local, mix, xt, ht, wt, mask = call(
        functools.partial(local_body, steps, order),
        [shape(x.shape, F32)] * 4
        + [square, turned, turned, shape((chans, chans), BF16), shape((regions - 1, tiles, 8, chans), F32)],
        [HB] * 7, "local",
        scratch=[
            pltpu.SMEM(neighbours.shape, jnp.int32), pltpu.VMEM(x.shape, BF16), pltpu.VMEM(x.shape, BF16),
            pltpu.VMEM(w_filter.shape, BF16), pltpu.VMEM(w_gate.shape, BF16), pltpu.VMEM(w_mix.shape, BF16),
            pltpu.VMEM(adjacency.shape, BF16), dma((7,)),
        ],
        flops=14 * block * chans, nbytes=30 * block,
    )(neighbours, x, cot, w_filter, w_gate, w_mix, adjacency)
    act_cot, sums, send = call(
        functools.partial(send_body, regions, steps),
        [shape((2,) + x.shape, BF16), shape(x.shape, BF16), shape((3, chans, chans), BF16)],
        [VM] * (9 + regions - 1), "send",
        flops=6 * block * chans, nbytes=30 * block,
    )(d_filter, d_gate, direct, local, mix, xt, ht, wt, mask, *arrived)
    swap = [(i, i ^ 1) for i in range(dp)]
    got = lax.ppermute(send, "dp", swap)
    keep, grad_inputs = call(
        functools.partial(keep_body, steps),
        [shape((3, chans, chans), F32), shape(x.shape, BF16)], [VM] * 8, "keep",
        flops=12 * block * chans, nbytes=30 * block,
    )(mix, xt, ht, act_cot, sums, cot, w_filter, w_gate)

    rows = chans // ways
    chunk = (3, rows, chans)

    def pairs(p, turn):
        result = []
        for d in range(dp):
            for r in range(regions):
                e, q = (d ^ (2 * p), r) if (d % 2 == 0) == turn else (d, r ^ p)
                result.append((d * regions + r, e * regions + q))
        return result

    own, *sends = call(
        functools.partial(split_body, ways),
        [shape(chunk, F32)] + [shape(chunk, BF16)] * (ways - 1), [VM] * 2, "split",
    )(keep, got)
    gots = [lax.ppermute(part, BOTH, pairs(p, True)) for p, part in enumerate(sends, 1)]
    (mine,) = call(add_body, [shape(chunk, BF16)], [VM] * ways, "add_first")(own, *gots)
    gots = [lax.ppermute(mine, BOTH, pairs(p, False)) for p in range(1, ways)]
    (done,) = call(add_body, [shape(chunk, BF16)], [VM] * ways, "add_second")(mine, *gots)
    chunks = [done] + [lax.ppermute(done, BOTH, pairs(p, True)) for p in range(1, ways)]
    others = [lax.ppermute(part, "dp", swap) for part in chunks]
    factor = 1.0 / math.sqrt(windows * dp * steps * sites * regions)
    results = [shape((2, chans, chans), F32)] * 3
    extra = dict(out_specs=[HB] * 3, scratch=[pltpu.VMEM((ways,) + chunk, F32), dma((ways, 3))])
    grads = call(functools.partial(scale_body, ways, factor, False), results, [VM] * ways, "scale_own", **extra)(*chunks)
    grads = call(
        functools.partial(scale_body, ways, factor, True), results, [VM] * ways + [HB] * 3, "scale_other",
        aliases={ways + a: a for a in range(3)}, **extra,
    )(*others, *grads)
    return (grad_inputs.reshape(inputs.shape), *grads)


def solution(mesh):
    return jax.shard_map(
        per_device,
        mesh=mesh,
        in_specs=(
            P("dp", None, "region", None),
            P("dp", None, "region", None),
            P(),
            P(),
            P(),
            P(),
            P("region", None, None, None),
        ),
        out_specs=(P("dp", None, "region", None), P(), P(), P()),
        check_vma=False,
    )
```

```python
import functools
import math

import jax
import jax.numpy as jnp
from jax import lax
from jax.experimental import pallas as pl
from jax.experimental.pallas import tpu as pltpu
from jax.sharding import PartitionSpec as P

TILE = 128
F32 = jnp.float32
BF16 = jnp.bfloat16
VM = pl.BlockSpec(memory_space=pltpu.VMEM)
HB = pl.BlockSpec(memory_space=pltpu.HBM)
BOTH = ("dp", "region")


def dot(a, b, ca=1, cb=0):
    return lax.dot_general(a, b, (((ca,), (cb,)), ((), ())), preferred_element_type=F32)


def call(body, outs, ins, name, out_specs=None, scratch=(), flops=0, nbytes=0, aliases=None):
    return pl.pallas_call(
        body,
        out_shape=outs,
        in_specs=ins,
        out_specs=out_specs or [VM] * len(outs),
        scratch_shapes=list(scratch),
        cost_estimate=pl.CostEstimate(flops=flops, bytes_accessed=nbytes, transcendentals=0),
        compiler_params=pltpu.CompilerParams(vmem_limit_bytes=40 * 1024 * 1024),
        input_output_aliases=aliases or {},
        name=name,
    )


def in_hbm(*arrays):
    return [pltpu.with_memory_space_constraint(array, pltpu.HBM) for array in arrays]


def fetch(pairs, sems):
    copies = [pltpu.make_async_copy(src, dst, sems.at[i]) for i, (src, dst) in enumerate(pairs)]
    for copy in copies:
        copy.start()
    return copies


def find_entry(nb_ref, source, target, tiles, per_tile):
    tile = jnp.int32(0)
    place = jnp.int32(0)
    named = jnp.int32(-1)
    for j in range(tiles):
        for k in range(per_tile):
            local = nb_ref[source * tiles + j, k] - target * tiles
            hit = jnp.logical_and(local >= 0, local < tiles)
            tile = jnp.where(hit, j, tile)
            place = jnp.where(hit, k, place)
            named = jnp.where(hit, local, named)
    return tile, place, named


def region_of():
    return lax.axis_index("region").astype(jnp.int32)


def lane_of():
    place = lax.axis_index("dp").astype(jnp.int32)
    lane, chip, region = jnp.bitwise_and(place, 1), lax.shift_right_logical(place, 1), region_of()
    return lane, jnp.where(lane == 0, chip, region), jnp.where(lane == 0, region, chip)


def outgoing_body(regions, order, nb_hbm, cot_hbm, adj_hbm, *refs):
    out_refs, (nb_ref, cot_ref, adj_ref, sems) = refs[: regions - 1], refs[regions - 1 :]
    me = region_of()
    tiles, per_tile = adj_ref.shape[:2]
    total = cot_ref.shape[0]
    parts = [(nb_hbm, nb_ref)]
    for j in range(tiles):
        rows = pl.ds(j * TILE, TILE)
        parts += [(cot_hbm.at[t, rows], cot_ref.at[t, rows]) for t in range(total)]
        parts += [(adj_hbm.at[j, pl.ds(k, 2)], adj_ref.at[j, pl.ds(k, 2)]) for k in range(0, per_tile, 2)]
    first, *copies = fetch(parts, sems)
    first.wait()
    found = [find_entry(nb_ref, me, jnp.bitwise_xor(me, p), tiles, per_tile) for p in order]
    for copy in copies:
        copy.wait()
    for out, (tile, place, _) in zip(out_refs, found):
        weights = adj_ref[tile, place]
        for t in range(total):
            rows = cot_ref[t, pl.ds(pl.multiple_of(tile * TILE, TILE), TILE), :]
            out[t] = dot(weights, rows, 0, 0).astype(BF16)


def local_body(
    steps, order, nb_hbm, x_hbm, cot_hbm, wf_hbm, wg_hbm, wm_hbm, adj_hbm,
    df_ref, dg_ref, direct_ref, local_ref, mix_ref, xt_ref, ht_ref, wt_ref, mask_ref,
    nb_ref, x_ref, cot_ref, wf_ref, wg_ref, wm_ref, adj_ref, sems,
):
    me = region_of()
    tiles, per_tile = adj_ref.shape[:2]
    total = cot_ref.shape[0]
    c_nb, c_x, c_wf, c_wg, c_cot, c_wm, c_adj = fetch(
        [(nb_hbm, nb_ref), (x_hbm, x_ref), (wf_hbm, wf_ref), (wg_hbm, wg_ref), (cot_hbm, cot_ref), (wm_hbm, wm_ref), (adj_hbm, adj_ref)],
        sems,
    )
    c_x.wait()
    c_wf.wait()
    c_wg.wait()
    for t in range(total):
        x = x_ref[t]
        act_f = dot(x, wf_ref[0])
        act_g = dot(x, wg_ref[0])
        if t % steps:
            before = x_ref[t - 1]
            act_f += dot(before, wf_ref[1])
            act_g += dot(before, wg_ref[1])
        filt = jnp.tanh(act_f)
        gate = jax.nn.sigmoid(act_g)
        both = filt * gate
        ht_ref[t] = both.astype(BF16).T
        xt_ref[t] = x.T
        df_ref[t] = gate * (1.0 - filt * filt)
        dg_ref[t] = both * (1.0 - gate)
    c_cot.wait()
    c_wm.wait()
    wt_ref[...] = wm_ref[1].T
    mix = jnp.zeros(mix_ref.shape, F32)
    for t in range(total):
        cot = cot_ref[t]
        direct_ref[t] = dot(cot, wm_ref[0], 1, 1)
        mix += dot(ht_ref[t], cot)
    mix_ref[...] = mix
    local_ref[...] = jnp.zeros_like(local_ref)
    c_nb.wait()
    c_adj.wait()
    for j in range(tiles):
        for k in range(per_tile):
            local = nb_ref[me * tiles + j, k] - me * tiles

            @pl.when(jnp.logical_and(local >= 0, local < tiles))
            def _():
                place = pl.ds(pl.multiple_of(local * TILE, TILE), TILE)
                for t in range(total):
                    local_ref[t, place, :] += dot(adj_ref[j, k], cot_ref[t, j * TILE : (j + 1) * TILE, :], 0, 0)

    for s, p in enumerate(order):
        _, _, named = find_entry(nb_ref, jnp.bitwise_xor(me, p), me, tiles, per_tile)
        for j in range(tiles):
            mask_ref[s, j] = jnp.full(mask_ref.shape[2:], jnp.where(named == j, 1.0, 0.0), F32)


def tap_rows(tap, part, steps, xt_ref, act_ref):
    total = xt_ref.shape[0]
    if tap == 0:
        terms = [dot(xt_ref[t], act_ref[part, t]) for t in range(total)]
    else:
        terms = [dot(xt_ref[t - 1], act_ref[part, t]) for t in range(total) if t % steps]
    return functools.reduce(jnp.add, terms)


def half_of(tap, steps, xt_ref, ht_ref, mix_ref, act_ref, sums_ref):
    if tap == 0:
        mix = mix_ref[...]
    else:
        mix = functools.reduce(jnp.add, [dot(ht_ref[t], sums_ref[t]) for t in range(ht_ref.shape[0])])
    return [tap_rows(tap, 0, steps, xt_ref, act_ref), tap_rows(tap, 1, steps, xt_ref, act_ref), mix]


def send_body(regions, steps, df_ref, dg_ref, direct_ref, local_ref, mix_ref, xt_ref, ht_ref, wt_ref, mask_ref, *refs):
    arrived, (act_ref, sums_ref, send_ref) = refs[: regions - 1], refs[regions - 1 :]
    lane, _, _ = lane_of()
    total, sites, _ = local_ref.shape
    tiles = sites // TILE
    for t in range(total):
        summed = []
        for j in range(tiles):
            part = local_ref[t, j * TILE : (j + 1) * TILE, :]
            for s in range(regions - 1):
                part += mask_ref[s, j, :1] * arrived[s][t].astype(F32)
            summed.append(part.astype(BF16))
        summed = jnp.concatenate(summed, axis=0)
        sums_ref[t] = summed
        grad = direct_ref[t] + dot(summed, wt_ref[...])
        act_ref[0, t] = (grad * df_ref[t]).astype(BF16)
        act_ref[1, t] = (grad * dg_ref[t]).astype(BF16)
    for tap in range(2):

        @pl.when(lane == 1 - tap)
        def _():
            for i, part in enumerate(half_of(tap, steps, xt_ref, ht_ref, mix_ref, act_ref, sums_ref)):
                send_ref[i] = part.astype(BF16)


def keep_body(steps, mix_ref, xt_ref, ht_ref, act_ref, sums_ref, cot_ref, wf_ref, wg_ref, keep_ref, out_ref):
    lane, _, _ = lane_of()
    for tap in range(2):

        @pl.when(lane == tap)
        def _():
            for i, part in enumerate(half_of(tap, steps, xt_ref, ht_ref, mix_ref, act_ref, sums_ref)):
                keep_ref[i] = part

    total = cot_ref.shape[0]
    for t in range(total):
        grad = cot_ref[t].astype(F32)
        grad += dot(act_ref[0, t], wf_ref[0], 1, 1) + dot(act_ref[1, t], wg_ref[0], 1, 1)
        if (t + 1) % steps:
            grad += dot(act_ref[0, t + 1], wf_ref[1], 1, 1) + dot(act_ref[1, t + 1], wg_ref[1], 1, 1)
        out_ref[t] = grad.astype(BF16)


def split_body(ways, keep_ref, got_ref, own_ref, *sends):
    _, mine, _ = lane_of()
    rows = own_ref.shape[1]

    def chunk(p):
        place = pl.ds(pl.multiple_of(jnp.bitwise_xor(mine, p) * rows, rows), rows)
        return keep_ref[:, place, :] + got_ref[:, place, :].astype(F32)

    own_ref[...] = chunk(0)
    for p, send in enumerate(sends, 1):
        send[...] = chunk(p).astype(BF16)


def tree(parts):
    while len(parts) > 1:
        parts = [parts[i] + parts[i + 1] for i in range(0, len(parts), 2)]
    return parts[0]


def add_body(*refs):
    refs[-1][...] = tree([ref[...].astype(F32) for ref in refs[:-1]]).astype(BF16)


def scale_body(ways, factor, other, *refs):
    chunks, refs = refs[:ways], refs[ways:]
    outs, (held, sems) = refs[-5:-2], refs[-2:]
    lane, first, second = lane_of()
    tap, mine = (1 - lane, second) if other else (lane, first)
    rows = chunks[0].shape[1]
    copies = []
    for p in range(ways):
        place = pl.ds(pl.multiple_of(jnp.bitwise_xor(mine, p) * rows, rows), rows)
        for a in range(3):
            held[p, a] = chunks[p][a].astype(F32) * factor
            copy = pltpu.make_async_copy(held.at[p, a], outs[a].at[tap, place], sems.at[p, a])
            copy.start()
            copies.append(copy)
    for copy in copies:
        copy.wait()


def per_device(inputs, cotangent, w_filter, w_gate, w_mix, neighbours, adjacency):
    regions = lax.axis_size("region")
    dp = lax.axis_size("dp")
    ways = dp // 2
    assert ways == regions
    windows, steps, sites, chans = inputs.shape
    total = windows * steps
    tiles, per_tile = adjacency.shape[:2]
    x = inputs.reshape(total, sites, chans)
    cot = cotangent.reshape(total, sites, chans)
    shape = jax.ShapeDtypeStruct
    block = total * sites * chans
    order = sorted(range(1, regions), reverse=True)
    dma = pltpu.SemaphoreType.DMA

    outgoing = call(
        functools.partial(outgoing_body, regions, order),
        [shape((total, TILE, chans), BF16)] * (regions - 1), [HB] * 3, "outgoing",
        scratch=[
            pltpu.SMEM(neighbours.shape, jnp.int32), pltpu.VMEM(cot.shape, BF16), pltpu.VMEM(adjacency.shape, BF16),
            dma((1 + tiles * (total + per_tile // 2),)),
        ],
        flops=2 * (regions - 1) * total * TILE * TILE * chans, nbytes=4 * block,
    )(*in_hbm(neighbours, cot, adjacency))
    arrived = [
        lax.ppermute(part, "region", [(r, r ^ p) for r in range(regions)]) for p, part in zip(order, outgoing)
    ]
    square = shape((chans, chans), F32)
    turned = shape((total, chans, sites), BF16)
    d_filter, d_gate, direct, local, mix, xt, ht, wt, mask = call(
        functools.partial(local_body, steps, order),
        [shape(x.shape, F32)] * 4
        + [square, turned, turned, shape((chans, chans), BF16), shape((regions - 1, tiles, 8, chans), F32)],
        [HB] * 7, "local",
        scratch=[
            pltpu.SMEM(neighbours.shape, jnp.int32), pltpu.VMEM(x.shape, BF16), pltpu.VMEM(x.shape, BF16),
            pltpu.VMEM(w_filter.shape, BF16), pltpu.VMEM(w_gate.shape, BF16), pltpu.VMEM(w_mix.shape, BF16),
            pltpu.VMEM(adjacency.shape, BF16), dma((7,)),
        ],
        flops=14 * block * chans, nbytes=30 * block,
    )(*in_hbm(neighbours, x, cot, w_filter, w_gate, w_mix, adjacency))
    act_cot, sums, send = call(
        functools.partial(send_body, regions, steps),
        [shape((2,) + x.shape, BF16), shape(x.shape, BF16), shape((3, chans, chans), BF16)],
        [VM] * (9 + regions - 1), "send",
        flops=6 * block * chans, nbytes=30 * block,
    )(d_filter, d_gate, direct, local, mix, xt, ht, wt, mask, *arrived)
    swap = [(i, i ^ 1) for i in range(dp)]
    got = lax.ppermute(send, "dp", swap)
    keep, grad_inputs = call(
        functools.partial(keep_body, steps),
        [shape((3, chans, chans), F32), shape(x.shape, BF16)], [VM] * 8, "keep",
        flops=12 * block * chans, nbytes=30 * block,
    )(mix, xt, ht, act_cot, sums, cot, w_filter, w_gate)

    rows = chans // ways
    chunk = (3, rows, chans)

    def pairs(p, turn):
        result = []
        for d in range(dp):
            for r in range(regions):
                e, q = (d ^ (2 * p), r) if (d % 2 == 0) == turn else (d, r ^ p)
                result.append((d * regions + r, e * regions + q))
        return result

    own, *sends = call(
        functools.partial(split_body, ways),
        [shape(chunk, F32)] + [shape(chunk, BF16)] * (ways - 1), [VM] * 2, "split",
    )(keep, got)
    gots = [lax.ppermute(part, BOTH, pairs(p, True)) for p, part in enumerate(sends, 1)]
    (mine,) = call(add_body, [shape(chunk, BF16)], [VM] * ways, "add_first")(own, *gots)
    gots = [lax.ppermute(mine, BOTH, pairs(p, False)) for p in range(1, ways)]
    (done,) = call(add_body, [shape(chunk, BF16)], [VM] * ways, "add_second")(mine, *gots)
    chunks = [done] + [lax.ppermute(done, BOTH, pairs(p, True)) for p in range(1, ways)]
    others = [lax.ppermute(part, "dp", swap) for part in chunks]
    factor = 1.0 / math.sqrt(windows * dp * steps * sites * regions)
    results = [shape((2, chans, chans), F32)] * 3
    extra = dict(out_specs=[HB] * 3, scratch=[pltpu.VMEM((ways,) + chunk, F32), dma((ways, 3))])
    grads = call(functools.partial(scale_body, ways, factor, False), results, [VM] * ways, "scale_own", **extra)(*chunks)
    grads = call(
        functools.partial(scale_body, ways, factor, True), results, [VM] * ways + [HB] * 3, "scale_other",
        aliases={ways + a: a for a in range(3)}, **extra,
    )(*others, *grads)
    return (grad_inputs.reshape(inputs.shape), *grads)


def solution(mesh):
    return jax.shard_map(
        per_device,
        mesh=mesh,
        in_specs=(
            P("dp", None, "region", None),
            P("dp", None, "region", None),
            P(),
            P(),
            P(),
            P(),
            P("region", None, None, None),
        ),
        out_specs=(P("dp", None, "region", None), P(), P(), P()),
        check_vma=False,
    )
```

```python
import functools
import math

import jax
import jax.numpy as jnp
from jax import lax
from jax.experimental import pallas as pl
from jax.experimental.pallas import tpu as pltpu
from jax.sharding import PartitionSpec as P

TILE = 128
F32 = jnp.float32
BF16 = jnp.bfloat16
VM = pl.BlockSpec(memory_space=pltpu.VMEM)
HB = pl.BlockSpec(memory_space=pltpu.HBM)
AN = pl.BlockSpec(memory_space=pl.ANY)
BOTH = ("dp", "region")


def dot(a, b, ca=1, cb=0):
    return lax.dot_general(a, b, (((ca,), (cb,)), ((), ())), preferred_element_type=F32)


def call(body, outs, ins, name, out_specs=None, scratch=(), flops=0, nbytes=0, aliases=None):
    return pl.pallas_call(
        body,
        out_shape=outs,
        in_specs=ins,
        out_specs=out_specs or [VM] * len(outs),
        scratch_shapes=list(scratch),
        cost_estimate=pl.CostEstimate(flops=flops, bytes_accessed=nbytes, transcendentals=0),
        compiler_params=pltpu.CompilerParams(vmem_limit_bytes=40 * 1024 * 1024),
        input_output_aliases=aliases or {},
        name=name,
    )


def in_hbm(*arrays):
    return [pltpu.with_memory_space_constraint(array, pltpu.HBM) for array in arrays]


def fetch(pairs, sems):
    copies = [pltpu.make_async_copy(src, dst, sems.at[i]) for i, (src, dst) in enumerate(pairs)]
    for copy in copies:
        copy.start()
    return copies


def find_entry(nb_ref, source, target, tiles, per_tile):
    tile = jnp.int32(0)
    place = jnp.int32(0)
    named = jnp.int32(-1)
    for j in range(tiles):
        for k in range(per_tile):
            local = nb_ref[source * tiles + j, k] - target * tiles
            hit = jnp.logical_and(local >= 0, local < tiles)
            tile = jnp.where(hit, j, tile)
            place = jnp.where(hit, k, place)
            named = jnp.where(hit, local, named)
    return tile, place, named


def region_of():
    return lax.axis_index("region").astype(jnp.int32)


def lane_of():
    place = lax.axis_index("dp").astype(jnp.int32)
    lane, chip, region = jnp.bitwise_and(place, 1), lax.shift_right_logical(place, 1), region_of()
    return lane, jnp.where(lane == 0, chip, region), jnp.where(lane == 0, region, chip)


def outgoing_body(regions, order, nb_hbm, cot_hbm, adj_hbm, *refs):
    out_refs, (nb_ref, cot_ref, adj_ref, sems) = refs[: regions - 1], refs[regions - 1 :]
    me = region_of()
    tiles, per_tile = adj_ref.shape[:2]
    total = cot_ref.shape[0]
    parts = [(nb_hbm, nb_ref)]
    for j in range(tiles):
        rows = pl.ds(j * TILE, TILE)
        parts += [(cot_hbm.at[t, rows], cot_ref.at[t, rows]) for t in range(total)]
        parts += [(adj_hbm.at[j, pl.ds(k, 2)], adj_ref.at[j, pl.ds(k, 2)]) for k in range(0, per_tile, 2)]
    first, *copies = fetch(parts, sems)
    first.wait()
    found = [find_entry(nb_ref, me, jnp.bitwise_xor(me, p), tiles, per_tile) for p in order]
    for copy in copies:
        copy.wait()
    for out, (tile, place, _) in zip(out_refs, found):
        weights = adj_ref[tile, place]
        for t in range(total):
            rows = cot_ref[t, pl.ds(pl.multiple_of(tile * TILE, TILE), TILE), :]
            out[t] = dot(weights, rows, 0, 0).astype(BF16)


def local_body(
    steps, order, nb_hbm, x_hbm, cot_hbm, wf_hbm, wg_hbm, wm_hbm, adj_hbm,
    df_ref, dg_ref, direct_ref, local_ref, mix_ref, xt_ref, ht_ref, wt_ref, mask_ref,
    nb_ref, x_ref, cot_ref, wf_ref, wg_ref, wm_ref, adj_ref, sems,
):
    me = region_of()
    tiles, per_tile = adj_ref.shape[:2]
    total = cot_ref.shape[0]
    c_nb, c_x, c_wf, c_wg, c_cot, c_wm, c_adj = fetch(
        [(nb_hbm, nb_ref), (x_hbm, x_ref), (wf_hbm, wf_ref), (wg_hbm, wg_ref), (cot_hbm, cot_ref), (wm_hbm, wm_ref), (adj_hbm, adj_ref)],
        sems,
    )
    c_x.wait()
    c_wf.wait()
    c_wg.wait()
    for t in range(total):
        x = x_ref[t]
        act_f = dot(x, wf_ref[0])
        act_g = dot(x, wg_ref[0])
        if t % steps:
            before = x_ref[t - 1]
            act_f += dot(before, wf_ref[1])
            act_g += dot(before, wg_ref[1])
        filt = jnp.tanh(act_f)
        gate = jax.nn.sigmoid(act_g)
        both = filt * gate
        ht_ref[t] = both.astype(BF16).T
        xt_ref[t] = x.T
        df_ref[t] = gate * (1.0 - filt * filt)
        dg_ref[t] = both * (1.0 - gate)
    c_cot.wait()
    c_wm.wait()
    wt_ref[...] = wm_ref[1].T
    mix = jnp.zeros(mix_ref.shape, F32)
    for t in range(total):
        cot = cot_ref[t]
        direct_ref[t] = dot(cot, wm_ref[0], 1, 1)
        mix += dot(ht_ref[t], cot)
    mix_ref[...] = mix
    local_ref[...] = jnp.zeros_like(local_ref)
    c_nb.wait()
    c_adj.wait()
    for j in range(tiles):
        for k in range(per_tile):
            local = nb_ref[me * tiles + j, k] - me * tiles

            @pl.when(jnp.logical_and(local >= 0, local < tiles))
            def _():
                place = pl.ds(pl.multiple_of(local * TILE, TILE), TILE)
                for t in range(total):
                    local_ref[t, place, :] += dot(adj_ref[j, k], cot_ref[t, j * TILE : (j + 1) * TILE, :], 0, 0)

    for s, p in enumerate(order):
        _, _, named = find_entry(nb_ref, jnp.bitwise_xor(me, p), me, tiles, per_tile)
        for j in range(tiles):
            mask_ref[s, j] = jnp.full(mask_ref.shape[2:], jnp.where(named == j, 1.0, 0.0), F32)


def tap_rows(tap, part, steps, xt_ref, act_ref):
    total = xt_ref.shape[0]
    if tap == 0:
        terms = [dot(xt_ref[t], act_ref[part, t]) for t in range(total)]
    else:
        terms = [dot(xt_ref[t - 1], act_ref[part, t]) for t in range(total) if t % steps]
    return functools.reduce(jnp.add, terms)


def half_of(tap, steps, xt_ref, ht_ref, mix_ref, act_ref, sums_ref):
    if tap == 0:
        mix = mix_ref[...]
    else:
        mix = functools.reduce(jnp.add, [dot(ht_ref[t], sums_ref[t]) for t in range(ht_ref.shape[0])])
    return [tap_rows(tap, 0, steps, xt_ref, act_ref), tap_rows(tap, 1, steps, xt_ref, act_ref), mix]


def send_body(regions, steps, df_ref, dg_ref, direct_ref, local_ref, mix_ref, xt_ref, ht_ref, wt_ref, mask_ref, *refs):
    arrived, (act_ref, sums_ref, send_ref) = refs[: regions - 1], refs[regions - 1 :]
    lane, _, _ = lane_of()
    total, sites, _ = local_ref.shape
    tiles = sites // TILE
    for t in range(total):
        summed = []
        for j in range(tiles):
            part = local_ref[t, j * TILE : (j + 1) * TILE, :]
            for s in range(regions - 1):
                part += mask_ref[s, j, :1] * arrived[s][t].astype(F32)
            summed.append(part.astype(BF16))
        summed = jnp.concatenate(summed, axis=0)
        sums_ref[t] = summed
        grad = direct_ref[t] + dot(summed, wt_ref[...])
        act_ref[0, t] = (grad * df_ref[t]).astype(BF16)
        act_ref[1, t] = (grad * dg_ref[t]).astype(BF16)
    for tap in range(2):

        @pl.when(lane == 1 - tap)
        def _():
            for i, part in enumerate(half_of(tap, steps, xt_ref, ht_ref, mix_ref, act_ref, sums_ref)):
                send_ref[i] = part.astype(BF16)


def keep_body(steps, mix_ref, xt_ref, ht_ref, act_ref, sums_ref, keep_ref):
    lane, _, _ = lane_of()
    for tap in range(2):

        @pl.when(lane == tap)
        def _():
            for i, part in enumerate(half_of(tap, steps, xt_ref, ht_ref, mix_ref, act_ref, sums_ref)):
                keep_ref[i] = part


def inputs_body(steps, act_ref, cot_ref, wf_ref, wg_ref, _, out_ref, token_ref):
    token_ref[...] = jnp.zeros_like(token_ref)
    total = cot_ref.shape[0]
    for t in range(total):
        grad = cot_ref[t].astype(F32)
        grad += dot(act_ref[0, t], wf_ref[0], 1, 1) + dot(act_ref[1, t], wg_ref[0], 1, 1)
        if (t + 1) % steps:
            grad += dot(act_ref[0, t + 1], wf_ref[1], 1, 1) + dot(act_ref[1, t + 1], wg_ref[1], 1, 1)
        out_ref[t] = grad.astype(BF16)


def split_body(ways, keep_ref, got_ref, own_ref, *sends):
    _, mine, _ = lane_of()
    rows = own_ref.shape[1]

    def chunk(p):
        place = pl.ds(pl.multiple_of(jnp.bitwise_xor(mine, p) * rows, rows), rows)
        return keep_ref[:, place, :] + got_ref[:, place, :].astype(F32)

    own_ref[...] = chunk(0)
    for p, send in enumerate(sends, 1):
        send[...] = chunk(p).astype(BF16)


def tree(parts):
    while len(parts) > 1:
        parts = [parts[i] + parts[i + 1] for i in range(0, len(parts), 2)]
    return parts[0]


def add_body(ways, *refs):
    refs[-1][...] = tree([ref[...].astype(F32) for ref in refs[:ways]]).astype(BF16)


def scale_body(ways, factor, other, *refs):
    chunks, refs = refs[:ways], refs[ways:]
    outs, (held, sems) = refs[-5:-2], refs[-2:]
    lane, first, second = lane_of()
    tap, mine = (1 - lane, second) if other else (lane, first)
    rows = chunks[0].shape[1]
    copies = []
    for p in range(ways):
        place = pl.ds(pl.multiple_of(jnp.bitwise_xor(mine, p) * rows, rows), rows)
        for a in range(3):
            held[p, a] = chunks[p][a].astype(F32) * factor
            copy = pltpu.make_async_copy(held.at[p, a], outs[a].at[tap, place], sems.at[p, a])
            copy.start()
            copies.append(copy)
    for copy in copies:
        copy.wait()


def per_device(inputs, cotangent, w_filter, w_gate, w_mix, neighbours, adjacency):
    regions = lax.axis_size("region")
    dp = lax.axis_size("dp")
    ways = dp // 2
    assert ways == regions
    windows, steps, sites, chans = inputs.shape
    total = windows * steps
    tiles, per_tile = adjacency.shape[:2]
    x = inputs.reshape(total, sites, chans)
    cot = cotangent.reshape(total, sites, chans)
    shape = jax.ShapeDtypeStruct
    block = total * sites * chans
    order = sorted(range(1, regions), key=lambda p: p != regions // 2)
    dma = pltpu.SemaphoreType.DMA

    outgoing = call(
        functools.partial(outgoing_body, regions, order),
        [shape((total, TILE, chans), BF16)] * (regions - 1), [HB] * 3, "outgoing",
        scratch=[
            pltpu.SMEM(neighbours.shape, jnp.int32), pltpu.VMEM(cot.shape, BF16), pltpu.VMEM(adjacency.shape, BF16),
            dma((1 + tiles * (total + per_tile // 2),)),
        ],
        flops=2 * (regions - 1) * total * TILE * TILE * chans, nbytes=4 * block,
    )(*in_hbm(neighbours, cot, adjacency))
    arrived = [
        lax.ppermute(part, "region", [(r, r ^ p) for r in range(regions)]) for p, part in zip(order, outgoing)
    ]
    square = shape((chans, chans), F32)
    turned = shape((total, chans, sites), BF16)
    d_filter, d_gate, direct, local, mix, xt, ht, wt, mask = call(
        functools.partial(local_body, steps, order),
        [shape(x.shape, F32)] * 4
        + [square, turned, turned, shape((chans, chans), BF16), shape((regions - 1, tiles, 8, chans), F32)],
        [HB] * 7, "local",
        scratch=[
            pltpu.SMEM(neighbours.shape, jnp.int32), pltpu.VMEM(x.shape, BF16), pltpu.VMEM(x.shape, BF16),
            pltpu.VMEM(w_filter.shape, BF16), pltpu.VMEM(w_gate.shape, BF16), pltpu.VMEM(w_mix.shape, BF16),
            pltpu.VMEM(adjacency.shape, BF16), dma((7,)),
        ],
        flops=14 * block * chans, nbytes=30 * block,
    )(*in_hbm(neighbours, x, cot, w_filter, w_gate, w_mix, adjacency))
    act_cot, sums, send = call(
        functools.partial(send_body, regions, steps),
        [shape((2,) + x.shape, BF16), shape(x.shape, BF16), shape((3, chans, chans), BF16)],
        [VM] * (9 + regions - 1), "send",
        flops=6 * block * chans, nbytes=30 * block,
    )(d_filter, d_gate, direct, local, mix, xt, ht, wt, mask, *arrived)
    swap = [(i, i ^ 1) for i in range(dp)]
    got = lax.ppermute(send, "dp", swap)
    (keep,) = call(
        functools.partial(keep_body, steps), [shape((3, chans, chans), F32)], [VM] * 5, "keep",
        flops=6 * block * chans, nbytes=20 * block,
    )(mix, xt, ht, act_cot, sums)

    rows = chans // ways
    chunk = (3, rows, chans)

    def pairs(p, turn):
        result = []
        for d in range(dp):
            for r in range(regions):
                e, q = (d ^ (2 * p), r) if (d % 2 == 0) == turn else (d, r ^ p)
                result.append((d * regions + r, e * regions + q))
        return result

    own, *sends = call(
        functools.partial(split_body, ways),
        [shape(chunk, F32)] + [shape(chunk, BF16)] * (ways - 1), [VM] * 2, "split",
    )(keep, got)
    gots = [lax.ppermute(part, BOTH, pairs(p, True)) for p, part in enumerate(sends, 1)]
    (mine,) = call(functools.partial(add_body, ways), [shape(chunk, BF16)], [VM] * ways, "add_first")(own, *gots)
    gots = [lax.ppermute(mine, BOTH, pairs(p, False)) for p in range(1, ways)]
    grad_inputs, token = call(
        functools.partial(inputs_body, steps), [shape(x.shape, BF16), shape((8, 128), F32)], [VM] * 4 + [AN], "inputs",
        flops=8 * block * chans, nbytes=16 * block,
    )(act_cot, cot, w_filter, w_gate, mine)
    (done,) = call(
        functools.partial(add_body, ways), [shape(chunk, BF16)], [VM] * ways + [AN], "add_second"
    )(mine, *gots, token)
    chunks = [done] + [lax.ppermute(done, BOTH, pairs(p, True)) for p in range(1, ways)]
    others = [lax.ppermute(part, "dp", swap) for part in chunks]
    factor = 1.0 / math.sqrt(windows * dp * steps * sites * regions)
    results = [shape((2, chans, chans), F32)] * 3
    extra = dict(out_specs=[HB] * 3, scratch=[pltpu.VMEM((ways,) + chunk, F32), dma((ways, 3))])
    grads = call(functools.partial(scale_body, ways, factor, False), results, [VM] * ways, "scale_own", **extra)(*chunks)
    grads = call(
        functools.partial(scale_body, ways, factor, True), results, [VM] * ways + [HB] * 3, "scale_other",
        aliases={ways + a: a for a in range(3)}, **extra,
    )(*others, *grads)
    return (grad_inputs.reshape(inputs.shape), *grads)


def solution(mesh):
    return jax.shard_map(
        per_device,
        mesh=mesh,
        in_specs=(
            P("dp", None, "region", None),
            P("dp", None, "region", None),
            P(),
            P(),
            P(),
            P(),
            P("region", None, None, None),
        ),
        out_specs=(P("dp", None, "region", None), P(), P(), P()),
        check_vma=False,
    )
```

```python
import functools
import math

import jax
import jax.numpy as jnp
from jax import lax
from jax.experimental import pallas as pl
from jax.experimental.pallas import tpu as pltpu
from jax.sharding import PartitionSpec as P

TILE = 128
F32 = jnp.float32
BF16 = jnp.bfloat16
VM = pl.BlockSpec(memory_space=pltpu.VMEM)
HB = pl.BlockSpec(memory_space=pltpu.HBM)
AN = pl.BlockSpec(memory_space=pl.ANY)
BOTH = ("dp", "region")


def dot(a, b, ca=1, cb=0):
    return lax.dot_general(a, b, (((ca,), (cb,)), ((), ())), preferred_element_type=F32)


def call(body, outs, ins, name, out_specs=None, scratch=(), flops=0, nbytes=0, aliases=None):
    return pl.pallas_call(
        body,
        out_shape=outs,
        in_specs=ins,
        out_specs=out_specs or [VM] * len(outs),
        scratch_shapes=list(scratch),
        cost_estimate=pl.CostEstimate(flops=flops, bytes_accessed=nbytes, transcendentals=0),
        compiler_params=pltpu.CompilerParams(vmem_limit_bytes=40 * 1024 * 1024),
        input_output_aliases=aliases or {},
        name=name,
    )


def in_hbm(*arrays):
    return [pltpu.with_memory_space_constraint(array, pltpu.HBM) for array in arrays]


def fetch(pairs, sems):
    copies = [pltpu.make_async_copy(src, dst, sems.at[i]) for i, (src, dst) in enumerate(pairs)]
    for copy in copies:
        copy.start()
    return copies


def find_entry(nb_ref, source, target, tiles, per_tile):
    tile = jnp.int32(0)
    place = jnp.int32(0)
    named = jnp.int32(-1)
    for j in range(tiles):
        for k in range(per_tile):
            local = nb_ref[source * tiles + j, k] - target * tiles
            hit = jnp.logical_and(local >= 0, local < tiles)
            tile = jnp.where(hit, j, tile)
            place = jnp.where(hit, k, place)
            named = jnp.where(hit, local, named)
    return tile, place, named


def region_of():
    return lax.axis_index("region").astype(jnp.int32)


def lane_of():
    place = lax.axis_index("dp").astype(jnp.int32)
    lane, chip, region = jnp.bitwise_and(place, 1), lax.shift_right_logical(place, 1), region_of()
    return lane, jnp.where(lane == 0, chip, region), jnp.where(lane == 0, region, chip)


def outgoing_body(regions, order, nb_hbm, cot_hbm, adj_hbm, *refs):
    out_refs, (nb_ref, cot_ref, adj_ref, sems) = refs[: regions - 1], refs[regions - 1 :]
    me = region_of()
    tiles, per_tile = adj_ref.shape[:2]
    total = cot_ref.shape[0]
    parts = [(nb_hbm, nb_ref), (cot_hbm, cot_ref), (adj_hbm, adj_ref)]
    first, *copies = fetch(parts, sems)
    first.wait()
    found = [find_entry(nb_ref, me, jnp.bitwise_xor(me, p), tiles, per_tile) for p in order]
    for copy in copies:
        copy.wait()
    for out, (tile, place, _) in zip(out_refs, found):
        weights = adj_ref[tile, place]
        for t in range(total):
            rows = cot_ref[t, pl.ds(pl.multiple_of(tile * TILE, TILE), TILE), :]
            out[t] = dot(weights, rows, 0, 0).astype(BF16)


def local_body(
    steps, order, nb_hbm, x_hbm, cot_hbm, wf_hbm, wg_hbm, wm_hbm, adj_hbm,
    df_ref, dg_ref, direct_ref, local_ref, mix_ref, xt_ref, ht_ref, wt_ref, mask_ref,
    nb_ref, x_ref, cot_ref, wf_ref, wg_ref, wm_ref, adj_ref, sems,
):
    me = region_of()
    tiles, per_tile = adj_ref.shape[:2]
    total = cot_ref.shape[0]
    c_nb, c_x, c_wf, c_wg, c_cot, c_wm, c_adj = fetch(
        [(nb_hbm, nb_ref), (x_hbm, x_ref), (wf_hbm, wf_ref), (wg_hbm, wg_ref), (cot_hbm, cot_ref), (wm_hbm, wm_ref), (adj_hbm, adj_ref)],
        sems,
    )
    c_x.wait()
    c_wf.wait()
    c_wg.wait()
    for t in range(total):
        x = x_ref[t]
        act_f = dot(x, wf_ref[0])
        act_g = dot(x, wg_ref[0])
        if t % steps:
            before = x_ref[t - 1]
            act_f += dot(before, wf_ref[1])
            act_g += dot(before, wg_ref[1])
        filt = jnp.tanh(act_f)
        gate = jax.nn.sigmoid(act_g)
        both = filt * gate
        ht_ref[t] = both.astype(BF16).T
        xt_ref[t] = x.T
        df_ref[t] = gate * (1.0 - filt * filt)
        dg_ref[t] = both * (1.0 - gate)
    c_cot.wait()
    c_wm.wait()
    wt_ref[...] = wm_ref[1].T
    mix = jnp.zeros(mix_ref.shape, F32)
    for t in range(total):
        cot = cot_ref[t]
        direct_ref[t] = dot(cot, wm_ref[0], 1, 1)
        mix += dot(ht_ref[t], cot)
    mix_ref[...] = mix
    local_ref[...] = jnp.zeros_like(local_ref)
    c_nb.wait()
    c_adj.wait()
    for j in range(tiles):
        for k in range(per_tile):
            local = nb_ref[me * tiles + j, k] - me * tiles

            @pl.when(jnp.logical_and(local >= 0, local < tiles))
            def _():
                place = pl.ds(pl.multiple_of(local * TILE, TILE), TILE)
                for t in range(total):
                    local_ref[t, place, :] += dot(adj_ref[j, k], cot_ref[t, j * TILE : (j + 1) * TILE, :], 0, 0)

    for s, p in enumerate(order):
        _, _, named = find_entry(nb_ref, jnp.bitwise_xor(me, p), me, tiles, per_tile)
        for j in range(tiles):
            mask_ref[s, j] = jnp.full(mask_ref.shape[2:], jnp.where(named == j, 1.0, 0.0), F32)


def tap_rows(tap, part, steps, xt_ref, act_ref):
    total = xt_ref.shape[0]
    if tap == 0:
        terms = [dot(xt_ref[t], act_ref[part, t]) for t in range(total)]
    else:
        terms = [dot(xt_ref[t - 1], act_ref[part, t]) for t in range(total) if t % steps]
    return functools.reduce(jnp.add, terms)


def half_of(tap, steps, xt_ref, ht_ref, mix_ref, act_ref, sums_ref):
    if tap == 0:
        mix = mix_ref[...]
    else:
        mix = functools.reduce(jnp.add, [dot(ht_ref[t], sums_ref[t]) for t in range(ht_ref.shape[0])])
    return [tap_rows(tap, 0, steps, xt_ref, act_ref), tap_rows(tap, 1, steps, xt_ref, act_ref), mix]


def send_body(regions, steps, df_ref, dg_ref, direct_ref, local_ref, mix_ref, xt_ref, ht_ref, wt_ref, mask_ref, *refs):
    arrived, (act_ref, sums_ref, send_ref) = refs[: regions - 1], refs[regions - 1 :]
    lane, _, _ = lane_of()
    total, sites, _ = local_ref.shape
    tiles = sites // TILE
    for t in range(total):
        summed = []
        for j in range(tiles):
            part = local_ref[t, j * TILE : (j + 1) * TILE, :]
            for s in range(regions - 1):
                part += mask_ref[s, j, :1] * arrived[s][t].astype(F32)
            summed.append(part.astype(BF16))
        summed = jnp.concatenate(summed, axis=0)
        sums_ref[t] = summed
        grad = direct_ref[t] + dot(summed, wt_ref[...])
        act_ref[0, t] = (grad * df_ref[t]).astype(BF16)
        act_ref[1, t] = (grad * dg_ref[t]).astype(BF16)
    for tap in range(2):

        @pl.when(lane == 1 - tap)
        def _():
            for i, part in enumerate(half_of(tap, steps, xt_ref, ht_ref, mix_ref, act_ref, sums_ref)):
                send_ref[i] = part.astype(BF16)


def keep_body(steps, mix_ref, xt_ref, ht_ref, act_ref, sums_ref, keep_ref):
    lane, _, _ = lane_of()
    for tap in range(2):

        @pl.when(lane == tap)
        def _():
            for i, part in enumerate(half_of(tap, steps, xt_ref, ht_ref, mix_ref, act_ref, sums_ref)):
                keep_ref[i] = part


def inputs_body(steps, act_ref, cot_ref, wf_ref, wg_ref, _, out_ref, token_ref):
    token_ref[...] = jnp.zeros_like(token_ref)
    total = cot_ref.shape[0]
    for t in range(total):
        grad = cot_ref[t].astype(F32)
        grad += dot(act_ref[0, t], wf_ref[0], 1, 1) + dot(act_ref[1, t], wg_ref[0], 1, 1)
        if (t + 1) % steps:
            grad += dot(act_ref[0, t + 1], wf_ref[1], 1, 1) + dot(act_ref[1, t + 1], wg_ref[1], 1, 1)
        out_ref[t] = grad.astype(BF16)


def split_body(ways, keep_ref, got_ref, own_ref, *sends):
    _, mine, _ = lane_of()
    rows = own_ref.shape[1]

    def chunk(p):
        place = pl.ds(pl.multiple_of(jnp.bitwise_xor(mine, p) * rows, rows), rows)
        return keep_ref[:, place, :] + got_ref[:, place, :].astype(F32)

    own_ref[...] = chunk(0)
    for p, send in enumerate(sends, 1):
        send[...] = chunk(p).astype(BF16)


def tree(parts):
    while len(parts) > 1:
        parts = [parts[i] + parts[i + 1] for i in range(0, len(parts), 2)]
    return parts[0]


def add_body(ways, *refs):
    refs[-1][...] = tree([ref[...].astype(F32) for ref in refs[:ways]]).astype(BF16)


def scale_body(ways, factor, other, *refs):
    chunks, refs = refs[:ways], refs[ways:]
    outs, (held, sems) = refs[-5:-2], refs[-2:]
    lane, first, second = lane_of()
    tap, mine = (1 - lane, second) if other else (lane, first)
    rows = chunks[0].shape[1]
    copies = []
    for p in range(ways):
        place = pl.ds(pl.multiple_of(jnp.bitwise_xor(mine, p) * rows, rows), rows)
        for a in range(3):
            held[p, a] = chunks[p][a].astype(F32) * factor
            copy = pltpu.make_async_copy(held.at[p, a], outs[a].at[tap, place], sems.at[p, a])
            copy.start()
            copies.append(copy)
    for copy in copies:
        copy.wait()


def per_device(inputs, cotangent, w_filter, w_gate, w_mix, neighbours, adjacency):
    regions = lax.axis_size("region")
    dp = lax.axis_size("dp")
    ways = dp // 2
    assert ways == regions
    windows, steps, sites, chans = inputs.shape
    total = windows * steps
    tiles, per_tile = adjacency.shape[:2]
    x = inputs.reshape(total, sites, chans)
    cot = cotangent.reshape(total, sites, chans)
    shape = jax.ShapeDtypeStruct
    block = total * sites * chans
    order = sorted(range(1, regions), key=lambda p: p != regions // 2)
    dma = pltpu.SemaphoreType.DMA

    outgoing = call(
        functools.partial(outgoing_body, regions, order),
        [shape((total, TILE, chans), BF16)] * (regions - 1), [HB] * 3, "outgoing",
        scratch=[
            pltpu.SMEM(neighbours.shape, jnp.int32), pltpu.VMEM(cot.shape, BF16), pltpu.VMEM(adjacency.shape, BF16),
            dma((3,)),
        ],
        flops=2 * (regions - 1) * total * TILE * TILE * chans, nbytes=4 * block,
    )(*in_hbm(neighbours, cot, adjacency))
    arrived = [
        lax.ppermute(part, "region", [(r, r ^ p) for r in range(regions)]) for p, part in zip(order, outgoing)
    ]
    square = shape((chans, chans), F32)
    turned = shape((total, chans, sites), BF16)
    d_filter, d_gate, direct, local, mix, xt, ht, wt, mask = call(
        functools.partial(local_body, steps, order),
        [shape(x.shape, F32)] * 4
        + [square, turned, turned, shape((chans, chans), BF16), shape((regions - 1, tiles, 8, chans), F32)],
        [HB] * 7, "local",
        scratch=[
            pltpu.SMEM(neighbours.shape, jnp.int32), pltpu.VMEM(x.shape, BF16), pltpu.VMEM(x.shape, BF16),
            pltpu.VMEM(w_filter.shape, BF16), pltpu.VMEM(w_gate.shape, BF16), pltpu.VMEM(w_mix.shape, BF16),
            pltpu.VMEM(adjacency.shape, BF16), dma((7,)),
        ],
        flops=14 * block * chans, nbytes=30 * block,
    )(*in_hbm(neighbours, x, cot, w_filter, w_gate, w_mix, adjacency))
    act_cot, sums, send = call(
        functools.partial(send_body, regions, steps),
        [shape((2,) + x.shape, BF16), shape(x.shape, BF16), shape((3, chans, chans), BF16)],
        [VM] * (9 + regions - 1), "send",
        flops=6 * block * chans, nbytes=30 * block,
    )(d_filter, d_gate, direct, local, mix, xt, ht, wt, mask, *arrived)
    swap = [(i, i ^ 1) for i in range(dp)]
    got = lax.ppermute(send, "dp", swap)
    (keep,) = call(
        functools.partial(keep_body, steps), [shape((3, chans, chans), F32)], [VM] * 5, "keep",
        flops=6 * block * chans, nbytes=20 * block,
    )(mix, xt, ht, act_cot, sums)

    rows = chans // ways
    chunk = (3, rows, chans)

    def pairs(p, turn):
        result = []
        for d in range(dp):
            for r in range(regions):
                e, q = (d ^ (2 * p), r) if (d % 2 == 0) == turn else (d, r ^ p)
                result.append((d * regions + r, e * regions + q))
        return result

    own, *sends = call(
        functools.partial(split_body, ways),
        [shape(chunk, F32)] + [shape(chunk, BF16)] * (ways - 1), [VM] * 2, "split",
    )(keep, got)
    gots = [lax.ppermute(part, BOTH, pairs(p, True)) for p, part in enumerate(sends, 1)]
    (mine,) = call(functools.partial(add_body, ways), [shape(chunk, BF16)], [VM] * ways, "add_first")(own, *gots)
    gots = [lax.ppermute(mine, BOTH, pairs(p, False)) for p in range(1, ways)]
    grad_inputs, token = call(
        functools.partial(inputs_body, steps), [shape(x.shape, BF16), shape((8, 128), F32)], [VM] * 4 + [AN], "inputs",
        flops=8 * block * chans, nbytes=16 * block,
    )(act_cot, cot, w_filter, w_gate, mine)
    (done,) = call(
        functools.partial(add_body, ways), [shape(chunk, BF16)], [VM] * ways + [AN], "add_second"
    )(mine, *gots, token)
    chunks = [done] + [lax.ppermute(done, BOTH, pairs(p, True)) for p in range(1, ways)]
    others = [lax.ppermute(part, "dp", swap) for part in chunks]
    factor = 1.0 / math.sqrt(windows * dp * steps * sites * regions)
    results = [shape((2, chans, chans), F32)] * 3
    extra = dict(out_specs=[HB] * 3, scratch=[pltpu.VMEM((ways,) + chunk, F32), dma((ways, 3))])
    grads = call(functools.partial(scale_body, ways, factor, False), results, [VM] * ways, "scale_own", **extra)(*chunks)
    grads = call(
        functools.partial(scale_body, ways, factor, True), results, [VM] * ways + [HB] * 3, "scale_other",
        aliases={ways + a: a for a in range(3)}, **extra,
    )(*others, *grads)
    return (grad_inputs.reshape(inputs.shape), *grads)


def solution(mesh):
    return jax.shard_map(
        per_device,
        mesh=mesh,
        in_specs=(
            P("dp", None, "region", None),
            P("dp", None, "region", None),
            P(),
            P(),
            P(),
            P(),
            P("region", None, None, None),
        ),
        out_specs=(P("dp", None, "region", None), P(), P(), P()),
        check_vma=False,
    )
```

```python
import functools
import math

import jax
import jax.numpy as jnp
from jax import lax
from jax.experimental import pallas as pl
from jax.experimental.pallas import tpu as pltpu
from jax.sharding import PartitionSpec as P

TILE = 128
F32 = jnp.float32
BF16 = jnp.bfloat16
VM = pl.BlockSpec(memory_space=pltpu.VMEM)
HB = pl.BlockSpec(memory_space=pltpu.HBM)
AN = pl.BlockSpec(memory_space=pl.ANY)
BOTH = ("dp", "region")


def dot(a, b, ca=1, cb=0):
    return lax.dot_general(a, b, (((ca,), (cb,)), ((), ())), preferred_element_type=F32)


def call(body, outs, ins, name, out_specs=None, scratch=(), flops=0, nbytes=0, aliases=None):
    return pl.pallas_call(
        body,
        out_shape=outs,
        in_specs=ins,
        out_specs=out_specs or [VM] * len(outs),
        scratch_shapes=list(scratch),
        cost_estimate=pl.CostEstimate(flops=flops, bytes_accessed=nbytes, transcendentals=0),
        compiler_params=pltpu.CompilerParams(vmem_limit_bytes=40 * 1024 * 1024),
        input_output_aliases=aliases or {},
        name=name,
    )


def in_hbm(*arrays):
    return [pltpu.with_memory_space_constraint(array, pltpu.HBM) for array in arrays]


def fetch(pairs, sems):
    copies = [pltpu.make_async_copy(src, dst, sems.at[i]) for i, (src, dst) in enumerate(pairs)]
    for copy in copies:
        copy.start()
    return copies


def find_entry(nb_ref, source, target, tiles, per_tile):
    tile = jnp.int32(0)
    place = jnp.int32(0)
    named = jnp.int32(-1)
    for j in range(tiles):
        for k in range(per_tile):
            local = nb_ref[source * tiles + j, k] - target * tiles
            hit = jnp.logical_and(local >= 0, local < tiles)
            tile = jnp.where(hit, j, tile)
            place = jnp.where(hit, k, place)
            named = jnp.where(hit, local, named)
    return tile, place, named


def region_of():
    return lax.axis_index("region").astype(jnp.int32)


def lane_of():
    place = lax.axis_index("dp").astype(jnp.int32)
    lane, chip, region = jnp.bitwise_and(place, 1), lax.shift_right_logical(place, 1), region_of()
    return lane, jnp.where(lane == 0, chip, region), jnp.where(lane == 0, region, chip)


def outgoing_body(regions, order, nb_hbm, cot_hbm, adj_hbm, *refs):
    out_refs, (nb_ref, cot_ref, adj_ref, sems) = refs[: regions - 1], refs[regions - 1 :]
    me = region_of()
    tiles, per_tile = adj_ref.shape[:2]
    total = cot_ref.shape[0]
    parts = [(nb_hbm, nb_ref), (cot_hbm, cot_ref), (adj_hbm, adj_ref)]
    first, *copies = fetch(parts, sems)
    first.wait()
    found = [find_entry(nb_ref, me, jnp.bitwise_xor(me, p), tiles, per_tile) for p in order]
    for copy in copies:
        copy.wait()
    for out, (tile, place, _) in zip(out_refs, found):
        weights = adj_ref[tile, place]
        for t in range(total):
            rows = cot_ref[t, pl.ds(pl.multiple_of(tile * TILE, TILE), TILE), :]
            out[t] = dot(weights, rows, 0, 0).astype(BF16)


def local_body(
    steps, order, nb_hbm, x_hbm, cot_hbm, wf_hbm, wg_hbm, wm_hbm, adj_hbm,
    df_ref, dg_ref, direct_ref, local_ref, mix_ref, xt_ref, ht_ref, wt_ref, mask_ref,
    nb_ref, x_ref, cot_ref, wf_ref, wg_ref, wm_ref, adj_ref, sems,
):
    me = region_of()
    tiles, per_tile = adj_ref.shape[:2]
    total = cot_ref.shape[0]
    c_nb, c_x, c_wf, c_wg, c_cot, c_wm, c_adj = fetch(
        [(nb_hbm, nb_ref), (x_hbm, x_ref), (wf_hbm, wf_ref), (wg_hbm, wg_ref), (cot_hbm, cot_ref), (wm_hbm, wm_ref), (adj_hbm, adj_ref)],
        sems,
    )
    c_x.wait()
    c_wf.wait()
    c_wg.wait()
    for t in range(total):
        x = x_ref[t]
        act_f = dot(x, wf_ref[0])
        act_g = dot(x, wg_ref[0])
        if t % steps:
            before = x_ref[t - 1]
            act_f += dot(before, wf_ref[1])
            act_g += dot(before, wg_ref[1])
        filt = jnp.tanh(act_f)
        gate = jax.nn.sigmoid(act_g)
        both = filt * gate
        ht_ref[t] = both.astype(BF16).T
        xt_ref[t] = x.T
        df_ref[t] = gate * (1.0 - filt * filt)
        dg_ref[t] = both * (1.0 - gate)
    c_cot.wait()
    c_wm.wait()
    wt_ref[...] = wm_ref[1].T
    mix = jnp.zeros(mix_ref.shape, F32)
    for t in range(total):
        cot = cot_ref[t]
        direct_ref[t] = dot(cot, wm_ref[0], 1, 1)
        mix += dot(ht_ref[t], cot)
    mix_ref[...] = mix
    local_ref[...] = jnp.zeros_like(local_ref)
    c_nb.wait()
    c_adj.wait()
    for j in range(tiles):
        for k in range(per_tile):
            local = nb_ref[me * tiles + j, k] - me * tiles

            @pl.when(jnp.logical_and(local >= 0, local < tiles))
            def _():
                place = pl.ds(pl.multiple_of(local * TILE, TILE), TILE)
                for t in range(total):
                    local_ref[t, place, :] += dot(adj_ref[j, k], cot_ref[t, j * TILE : (j + 1) * TILE, :], 0, 0)

    for s, p in enumerate(order):
        _, _, named = find_entry(nb_ref, jnp.bitwise_xor(me, p), me, tiles, per_tile)
        for j in range(tiles):
            mask_ref[s, j] = jnp.full(mask_ref.shape[2:], jnp.where(named == j, 1.0, 0.0), F32)


def tap_rows(tap, part, steps, xt_ref, act_ref):
    total = xt_ref.shape[0]
    if tap == 0:
        terms = [dot(xt_ref[t], act_ref[part, t]) for t in range(total)]
    else:
        terms = [dot(xt_ref[t - 1], act_ref[part, t]) for t in range(total) if t % steps]
    return functools.reduce(jnp.add, terms)


def half_of(tap, steps, xt_ref, ht_ref, mix_ref, act_ref, sums_ref):
    if tap == 0:
        mix = mix_ref[...]
    else:
        mix = functools.reduce(jnp.add, [dot(ht_ref[t], sums_ref[t]) for t in range(ht_ref.shape[0])])
    return [tap_rows(tap, 0, steps, xt_ref, act_ref), tap_rows(tap, 1, steps, xt_ref, act_ref), mix]


def send_body(regions, steps, df_ref, dg_ref, direct_ref, local_ref, mix_ref, xt_ref, ht_ref, wt_ref, mask_ref, *refs):
    arrived, (act_ref, sums_ref, send_ref) = refs[: regions - 1], refs[regions - 1 :]
    lane, _, _ = lane_of()
    total, sites, _ = local_ref.shape
    tiles = sites // TILE
    for t in range(total):
        summed = []
        for j in range(tiles):
            part = local_ref[t, j * TILE : (j + 1) * TILE, :]
            for s in range(regions - 1):
                part += mask_ref[s, j, :1] * arrived[s][t].astype(F32)
            summed.append(part.astype(BF16))
        summed = jnp.concatenate(summed, axis=0)
        sums_ref[t] = summed
        grad = direct_ref[t] + dot(summed, wt_ref[...])
        act_ref[0, t] = (grad * df_ref[t]).astype(BF16)
        act_ref[1, t] = (grad * dg_ref[t]).astype(BF16)
    for tap in range(2):

        @pl.when(lane == 1 - tap)
        def _():
            for i, part in enumerate(half_of(tap, steps, xt_ref, ht_ref, mix_ref, act_ref, sums_ref)):
                send_ref[i] = part.astype(BF16)


def keep_body(steps, mix_ref, xt_ref, ht_ref, act_ref, sums_ref, keep_ref):
    lane, _, _ = lane_of()
    for tap in range(2):

        @pl.when(lane == tap)
        def _():
            for i, part in enumerate(half_of(tap, steps, xt_ref, ht_ref, mix_ref, act_ref, sums_ref)):
                keep_ref[i] = part


def inputs_body(steps, act_ref, cot_ref, wf_ref, wg_ref, _, out_ref, token_ref):
    token_ref[...] = jnp.zeros_like(token_ref)
    total = cot_ref.shape[0]
    for t in range(total):
        grad = cot_ref[t].astype(F32)
        grad += dot(act_ref[0, t], wf_ref[0], 1, 1) + dot(act_ref[1, t], wg_ref[0], 1, 1)
        if (t + 1) % steps:
            grad += dot(act_ref[0, t + 1], wf_ref[1], 1, 1) + dot(act_ref[1, t + 1], wg_ref[1], 1, 1)
        out_ref[t] = grad.astype(BF16)


def split_body(ways, keep_ref, got_ref, own_ref, *sends):
    _, mine, _ = lane_of()
    rows = own_ref.shape[1]

    def chunk(p):
        place = pl.ds(pl.multiple_of(jnp.bitwise_xor(mine, p) * rows, rows), rows)
        return keep_ref[:, place, :] + got_ref[:, place, :].astype(F32)

    own_ref[...] = chunk(0)
    for p, send in enumerate(sends, 1):
        send[...] = chunk(p).astype(BF16)


def tree(parts):
    while len(parts) > 1:
        parts = [parts[i] + parts[i + 1] for i in range(0, len(parts), 2)]
    return parts[0]


def add_body(ways, *refs):
    refs[-1][...] = tree([ref[...].astype(F32) for ref in refs[:ways]]).astype(BF16)


def scale_body(ways, factor, other, *refs):
    chunks, refs = refs[:ways], refs[ways:]
    outs, (held, sems) = refs[-5:-2], refs[-2:]
    lane, first, second = lane_of()
    tap, mine = (1 - lane, second) if other else (lane, first)
    rows = chunks[0].shape[1]
    copies = []
    for p in range(ways):
        place = pl.ds(pl.multiple_of(jnp.bitwise_xor(mine, p) * rows, rows), rows)
        for a in range(3):
            held[p, a] = chunks[p][a].astype(F32) * factor
            copy = pltpu.make_async_copy(held.at[p, a], outs[a].at[tap, place], sems.at[p, a])
            copy.start()
            copies.append(copy)
    for copy in copies:
        copy.wait()


def per_device(inputs, cotangent, w_filter, w_gate, w_mix, neighbours, adjacency):
    regions = lax.axis_size("region")
    dp = lax.axis_size("dp")
    ways = dp // 2
    assert ways == regions
    windows, steps, sites, chans = inputs.shape
    total = windows * steps
    tiles, per_tile = adjacency.shape[:2]
    x = inputs.reshape(total, sites, chans)
    cot = cotangent.reshape(total, sites, chans)
    shape = jax.ShapeDtypeStruct
    block = total * sites * chans
    order = sorted(range(1, regions), key=lambda p: p != regions // 2)
    dma = pltpu.SemaphoreType.DMA

    outgoing = call(
        functools.partial(outgoing_body, regions, order),
        [shape((total, TILE, chans), BF16)] * (regions - 1), [HB] * 3, "outgoing",
        scratch=[
            pltpu.SMEM(neighbours.shape, jnp.int32), pltpu.VMEM(cot.shape, BF16), pltpu.VMEM(adjacency.shape, BF16),
            dma((3,)),
        ],
        flops=2 * (regions - 1) * total * TILE * TILE * chans, nbytes=4 * block,
    )(*in_hbm(neighbours, cot, adjacency))
    arrived = [
        lax.ppermute(part, "region", [(r, r ^ p) for r in range(regions)]) for p, part in zip(order, outgoing)
    ]
    square = shape((chans, chans), F32)
    turned = shape((total, chans, sites), BF16)
    d_filter, d_gate, direct, local, mix, xt, ht, wt, mask = call(
        functools.partial(local_body, steps, order),
        [shape(x.shape, F32)] * 4
        + [square, turned, turned, shape((chans, chans), BF16), shape((regions - 1, tiles, 8, chans), F32)],
        [HB] * 7, "local",
        scratch=[
            pltpu.SMEM(neighbours.shape, jnp.int32), pltpu.VMEM(x.shape, BF16), pltpu.VMEM(x.shape, BF16),
            pltpu.VMEM(w_filter.shape, BF16), pltpu.VMEM(w_gate.shape, BF16), pltpu.VMEM(w_mix.shape, BF16),
            pltpu.VMEM(adjacency.shape, BF16), dma((7,)),
        ],
        flops=14 * block * chans, nbytes=30 * block,
    )(*in_hbm(neighbours, x, cot, w_filter, w_gate, w_mix, adjacency))
    act_cot, sums, send = call(
        functools.partial(send_body, regions, steps),
        [shape((2,) + x.shape, BF16), shape(x.shape, BF16), shape((3, chans, chans), BF16)],
        [VM] * (9 + regions - 1), "send",
        flops=6 * block * chans, nbytes=30 * block,
    )(d_filter, d_gate, direct, local, mix, xt, ht, wt, mask, *arrived)
    swap = [(i, i ^ 1) for i in range(dp)]
    got = lax.ppermute(send, "dp", swap)
    (keep,) = call(
        functools.partial(keep_body, steps), [shape((3, chans, chans), F32)], [VM] * 5, "keep",
        flops=6 * block * chans, nbytes=20 * block,
    )(mix, xt, ht, act_cot, sums)

    rows = chans // ways
    chunk = (3, rows, chans)

    def pairs(p, turn):
        result = []
        for d in range(dp):
            for r in range(regions):
                e, q = (d ^ (2 * p), r) if (d % 2 == 0) == turn else (d, r ^ p)
                result.append((d * regions + r, e * regions + q))
        return result

    own, *sends = call(
        functools.partial(split_body, ways),
        [shape(chunk, F32)] + [shape(chunk, BF16)] * (ways - 1), [VM] * 2, "split",
    )(keep, got)
    gots = [lax.ppermute(part, BOTH, pairs(p, True)) for p, part in enumerate(sends, 1)]
    (mine,) = call(functools.partial(add_body, ways), [shape(chunk, BF16)], [VM] * ways, "add_first")(own, *gots)
    gots = [lax.ppermute(mine, BOTH, pairs(p, False)) for p in range(1, ways)]
    grad_inputs, token = call(
        functools.partial(inputs_body, steps), [shape(x.shape, BF16), shape((8, 128), F32)], [VM] * 4 + [AN], "inputs",
        flops=8 * block * chans, nbytes=16 * block,
    )(act_cot, cot, w_filter, w_gate, mine)
    (done,) = call(
        functools.partial(add_body, ways), [shape(chunk, BF16)], [VM] * ways + [AN], "add_second"
    )(mine, *gots, token)
    chunks = [done] + [lax.ppermute(done, BOTH, pairs(p, True)) for p in range(1, ways)]
    crossed = lax.ppermute(done, BOTH, [(i, j ^ regions) for i, j in pairs(1, True)])
    others = [crossed if i == 1 else lax.ppermute(part, "dp", swap) for i, part in enumerate(chunks)]
    factor = 1.0 / math.sqrt(windows * dp * steps * sites * regions)
    results = [shape((2, chans, chans), F32)] * 3
    extra = dict(out_specs=[HB] * 3, scratch=[pltpu.VMEM((ways,) + chunk, F32), dma((ways, 3))])
    grads = call(functools.partial(scale_body, ways, factor, False), results, [VM] * ways, "scale_own", **extra)(*chunks)
    grads = call(
        functools.partial(scale_body, ways, factor, True), results, [VM] * ways + [HB] * 3, "scale_other",
        aliases={ways + a: a for a in range(3)}, **extra,
    )(*others, *grads)
    return (grad_inputs.reshape(inputs.shape), *grads)


def solution(mesh):
    return jax.shard_map(
        per_device,
        mesh=mesh,
        in_specs=(
            P("dp", None, "region", None),
            P("dp", None, "region", None),
            P(),
            P(),
            P(),
            P(),
            P("region", None, None, None),
        ),
        out_specs=(P("dp", None, "region", None), P(), P(), P()),
        check_vma=False,
    )
```

```python
import functools
import math

import jax
import jax.numpy as jnp
from jax import lax
from jax.experimental import pallas as pl
from jax.experimental.pallas import tpu as pltpu
from jax.sharding import PartitionSpec as P

TILE = 128
F32 = jnp.float32
BF16 = jnp.bfloat16
VM = pl.BlockSpec(memory_space=pltpu.VMEM)
HB = pl.BlockSpec(memory_space=pltpu.HBM)
AN = pl.BlockSpec(memory_space=pl.ANY)
BOTH = ("dp", "region")


def dot(a, b, ca=1, cb=0):
    return lax.dot_general(a, b, (((ca,), (cb,)), ((), ())), preferred_element_type=F32)


def call(body, outs, ins, name, out_specs=None, scratch=(), flops=0, nbytes=0, aliases=None):
    return pl.pallas_call(
        body,
        out_shape=outs,
        in_specs=ins,
        out_specs=out_specs or [VM] * len(outs),
        scratch_shapes=list(scratch),
        cost_estimate=pl.CostEstimate(flops=flops, bytes_accessed=nbytes, transcendentals=0),
        compiler_params=pltpu.CompilerParams(vmem_limit_bytes=40 * 1024 * 1024),
        input_output_aliases=aliases or {},
        name=name,
    )


def in_hbm(*arrays):
    return [pltpu.with_memory_space_constraint(array, pltpu.HBM) for array in arrays]


def fetch(pairs, sems):
    copies = [pltpu.make_async_copy(src, dst, sems.at[i]) for i, (src, dst) in enumerate(pairs)]
    for copy in copies:
        copy.start()
    return copies


def find_entry(nb_ref, source, target, tiles, per_tile):
    tile = jnp.int32(0)
    place = jnp.int32(0)
    named = jnp.int32(-1)
    for j in range(tiles):
        for k in range(per_tile):
            local = nb_ref[source * tiles + j, k] - target * tiles
            hit = jnp.logical_and(local >= 0, local < tiles)
            tile = jnp.where(hit, j, tile)
            place = jnp.where(hit, k, place)
            named = jnp.where(hit, local, named)
    return tile, place, named


def region_of():
    return lax.axis_index("region").astype(jnp.int32)


def lane_of():
    place = lax.axis_index("dp").astype(jnp.int32)
    lane, chip, region = jnp.bitwise_and(place, 1), lax.shift_right_logical(place, 1), region_of()
    return lane, jnp.where(lane == 0, chip, region), jnp.where(lane == 0, region, chip)


def outgoing_body(regions, order, nb_hbm, cot_hbm, adj_hbm, *refs):
    out_refs, (nb_ref, cot_ref, adj_ref, sems) = refs[: regions - 1], refs[regions - 1 :]
    me = region_of()
    tiles, per_tile = adj_ref.shape[:2]
    total = cot_ref.shape[0]
    parts = [(nb_hbm, nb_ref), (cot_hbm, cot_ref), (adj_hbm, adj_ref)]
    first, *copies = fetch(parts, sems)
    first.wait()
    found = [find_entry(nb_ref, me, jnp.bitwise_xor(me, p), tiles, per_tile) for p in order]
    for copy in copies:
        copy.wait()
    for out, (tile, place, _) in zip(out_refs, found):
        weights = adj_ref[tile, place]
        for t in range(total):
            rows = cot_ref[t, pl.ds(pl.multiple_of(tile * TILE, TILE), TILE), :]
            out[t] = dot(weights, rows, 0, 0).astype(BF16)


def local_body(
    steps, order, nb_hbm, x_hbm, cot_hbm, wf_hbm, wg_hbm, wm_hbm, adj_hbm,
    df_ref, dg_ref, direct_ref, local_ref, mix_ref, xt_ref, ht_ref, wt_ref, mask_ref,
    nb_ref, x_ref, cot_ref, wf_ref, wg_ref, wm_ref, adj_ref, sems,
):
    me = region_of()
    tiles, per_tile = adj_ref.shape[:2]
    total = cot_ref.shape[0]
    c_nb, c_x, c_wf, c_wg, c_cot, c_wm, c_adj = fetch(
        [(nb_hbm, nb_ref), (x_hbm, x_ref), (wf_hbm, wf_ref), (wg_hbm, wg_ref), (cot_hbm, cot_ref), (wm_hbm, wm_ref), (adj_hbm, adj_ref)],
        sems,
    )
    c_x.wait()
    c_wf.wait()
    c_wg.wait()
    for t in range(total):
        x = x_ref[t]
        act_f = dot(x, wf_ref[0])
        act_g = dot(x, wg_ref[0])
        if t % steps:
            before = x_ref[t - 1]
            act_f += dot(before, wf_ref[1])
            act_g += dot(before, wg_ref[1])
        filt = jnp.tanh(act_f)
        gate = jax.nn.sigmoid(act_g)
        both = filt * gate
        ht_ref[t] = both.astype(BF16).T
        xt_ref[t] = x.T
        df_ref[t] = gate * (1.0 - filt * filt)
        dg_ref[t] = both * (1.0 - gate)
    c_cot.wait()
    c_wm.wait()
    wt_ref[...] = wm_ref[1].T
    mix = jnp.zeros(mix_ref.shape, F32)
    for t in range(total):
        cot = cot_ref[t]
        direct_ref[t] = dot(cot, wm_ref[0], 1, 1)
        mix += dot(ht_ref[t], cot)
    mix_ref[...] = mix
    local_ref[...] = jnp.zeros_like(local_ref)
    c_nb.wait()
    c_adj.wait()
    for j in range(tiles):
        for k in range(per_tile):
            local = nb_ref[me * tiles + j, k] - me * tiles

            @pl.when(jnp.logical_and(local >= 0, local < tiles))
            def _():
                place = pl.ds(pl.multiple_of(local * TILE, TILE), TILE)
                for t in range(total):
                    local_ref[t, place, :] += dot(adj_ref[j, k], cot_ref[t, j * TILE : (j + 1) * TILE, :], 0, 0)

    for s, p in enumerate(order):
        _, _, named = find_entry(nb_ref, jnp.bitwise_xor(me, p), me, tiles, per_tile)
        for j in range(tiles):
            mask_ref[s, j] = jnp.full(mask_ref.shape[2:], jnp.where(named == j, 1.0, 0.0), F32)


def tap_rows(tap, part, steps, xt_ref, act_ref):
    total = xt_ref.shape[0]
    if tap == 0:
        terms = [dot(xt_ref[t], act_ref[part, t]) for t in range(total)]
    else:
        terms = [dot(xt_ref[t - 1], act_ref[part, t]) for t in range(total) if t % steps]
    return functools.reduce(jnp.add, terms)


def chunk_of(ref, mine, p, rows):
    return ref[:, pl.ds(pl.multiple_of(jnp.bitwise_xor(mine, p) * rows, rows), rows), :]


def swapped(ref):
    return [0, *range(2, ref.shape[0] + 1)]


def half_of(tap, steps, xt_ref, ht_ref, mix_ref, act_ref, sums_ref):
    if tap == 0:
        mix = mix_ref[...]
    else:
        mix = functools.reduce(jnp.add, [dot(ht_ref[t], sums_ref[t]) for t in range(ht_ref.shape[0])])
    return [tap_rows(tap, 0, steps, xt_ref, act_ref), tap_rows(tap, 1, steps, xt_ref, act_ref), mix]


def send_body(regions, steps, df_ref, dg_ref, direct_ref, local_ref, mix_ref, xt_ref, ht_ref, wt_ref, mask_ref, *refs):
    arrived, (act_ref, sums_ref, cross_ref, rest_ref, made_ref) = refs[: regions - 1], refs[regions - 1 :]
    lane, _, other = lane_of()
    total, sites, _ = local_ref.shape
    tiles = sites // TILE
    for t in range(total):
        summed = []
        for j in range(tiles):
            part = local_ref[t, j * TILE : (j + 1) * TILE, :]
            for s in range(regions - 1):
                part += (mask_ref[s, j, :1].astype(BF16) * arrived[s][t]).astype(F32)
            summed.append(part.astype(BF16))
        summed = jnp.concatenate(summed, axis=0)
        sums_ref[t] = summed
        grad = direct_ref[t] + dot(summed, wt_ref[...])
        act_ref[0, t] = (grad * df_ref[t]).astype(BF16)
        act_ref[1, t] = (grad * dg_ref[t]).astype(BF16)
    for tap in range(2):

        @pl.when(lane == 1 - tap)
        def _():
            for i, part in enumerate(half_of(tap, steps, xt_ref, ht_ref, mix_ref, act_ref, sums_ref)):
                made_ref[i] = part

    rows = cross_ref.shape[1]
    cross_ref[...] = chunk_of(made_ref, other, 1, rows).astype(BF16)
    for i, p in enumerate(swapped(rest_ref)):
        rest_ref[i] = chunk_of(made_ref, other, p, rows).astype(BF16)


def keep_body(steps, mix_ref, xt_ref, ht_ref, act_ref, sums_ref, keep_ref, along_ref):
    lane, mine, _ = lane_of()
    for tap in range(2):

        @pl.when(lane == tap)
        def _():
            for i, part in enumerate(half_of(tap, steps, xt_ref, ht_ref, mix_ref, act_ref, sums_ref)):
                keep_ref[i] = part
    along_ref[...] = chunk_of(keep_ref, mine, 1, along_ref.shape[1]).astype(BF16)


def inputs_body(steps, act_ref, cot_ref, wf_ref, wg_ref, _, out_ref, token_ref):
    token_ref[...] = jnp.zeros_like(token_ref)
    total = cot_ref.shape[0]
    for t in range(total):
        grad = cot_ref[t].astype(F32)
        grad += dot(act_ref[0, t], wf_ref[0], 1, 1) + dot(act_ref[1, t], wg_ref[0], 1, 1)
        if (t + 1) % steps:
            grad += dot(act_ref[0, t + 1], wf_ref[1], 1, 1) + dot(act_ref[1, t + 1], wg_ref[1], 1, 1)
        out_ref[t] = grad.astype(BF16)


def split_body(keep_ref, got_ref, cross_ref, own_ref, *sends):
    _, mine, _ = lane_of()
    sends[-1][...] = cross_ref[...]
    for i, p in enumerate(swapped(got_ref)):
        part = chunk_of(keep_ref, mine, p, own_ref.shape[1]) + got_ref[i].astype(F32)
        if i == 0:
            own_ref[...] = part
        else:
            sends[i - 1][...] = part.astype(BF16)


def tree(parts):
    while len(parts) > 1:
        parts = [parts[i] + parts[i + 1] for i in range(0, len(parts), 2)]
    return parts[0]


def sum_body(*refs):
    refs[-1][...] = functools.reduce(jnp.add, [ref[...].astype(F32) for ref in refs[:-1]]).astype(BF16)


def add_body(ways, *refs):
    refs[-1][...] = tree([ref[...].astype(F32) for ref in refs[:ways]]).astype(BF16)


def scale_body(ways, factor, other, *refs):
    chunks, refs = refs[:ways], refs[ways:]
    outs, (held, sems) = refs[-5:-2], refs[-2:]
    lane, first, second = lane_of()
    tap, mine = (1 - lane, second) if other else (lane, first)
    rows = chunks[0].shape[1]
    copies = []
    for p in range(ways):
        place = pl.ds(pl.multiple_of(jnp.bitwise_xor(mine, p) * rows, rows), rows)
        for a in range(3):
            held[p, a] = chunks[p][a].astype(F32) * factor
            copy = pltpu.make_async_copy(held.at[p, a], outs[a].at[tap, place], sems.at[p, a])
            copy.start()
            copies.append(copy)
    for copy in copies:
        copy.wait()


def per_device(inputs, cotangent, w_filter, w_gate, w_mix, neighbours, adjacency):
    regions = lax.axis_size("region")
    dp = lax.axis_size("dp")
    ways = dp // 2
    assert ways == regions
    windows, steps, sites, chans = inputs.shape
    total = windows * steps
    tiles, per_tile = adjacency.shape[:2]
    x = inputs.reshape(total, sites, chans)
    cot = cotangent.reshape(total, sites, chans)
    shape = jax.ShapeDtypeStruct
    block = total * sites * chans
    order = sorted(range(1, regions), key=lambda p: p != regions // 2)
    dma = pltpu.SemaphoreType.DMA

    outgoing = call(
        functools.partial(outgoing_body, regions, order),
        [shape((total, TILE, chans), BF16)] * (regions - 1), [HB] * 3, "outgoing",
        scratch=[
            pltpu.SMEM(neighbours.shape, jnp.int32), pltpu.VMEM(cot.shape, BF16), pltpu.VMEM(adjacency.shape, BF16),
            dma((3,)),
        ],
        flops=2 * (regions - 1) * total * TILE * TILE * chans, nbytes=4 * block,
    )(*in_hbm(neighbours, cot, adjacency))
    arrived = [
        lax.ppermute(part, "region", [(r, r ^ p) for r in range(regions)]) for p, part in zip(order, outgoing)
    ]
    square = shape((chans, chans), F32)
    turned = shape((total, chans, sites), BF16)
    d_filter, d_gate, direct, local, mix, xt, ht, wt, mask = call(
        functools.partial(local_body, steps, order),
        [shape(x.shape, F32)] * 4
        + [square, turned, turned, shape((chans, chans), BF16), shape((regions - 1, tiles, 8, chans), F32)],
        [HB] * 7, "local",
        scratch=[
            pltpu.SMEM(neighbours.shape, jnp.int32), pltpu.VMEM(x.shape, BF16), pltpu.VMEM(x.shape, BF16),
            pltpu.VMEM(w_filter.shape, BF16), pltpu.VMEM(w_gate.shape, BF16), pltpu.VMEM(w_mix.shape, BF16),
            pltpu.VMEM(adjacency.shape, BF16), dma((7,)),
        ],
        flops=14 * block * chans, nbytes=30 * block,
    )(*in_hbm(neighbours, x, cot, w_filter, w_gate, w_mix, adjacency))
    rows = chans // ways
    chunk = (3, rows, chans)
    act_cot, sums, cross, rest = call(
        functools.partial(send_body, regions, steps),
        [shape((2,) + x.shape, BF16), shape(x.shape, BF16), shape(chunk, BF16), shape((ways - 1,) + chunk, BF16)],
        [VM] * (9 + regions - 1), "send", scratch=[pltpu.VMEM((3, chans, chans), F32)],
        flops=6 * block * chans, nbytes=30 * block,
    )(d_filter, d_gate, direct, local, mix, xt, ht, wt, mask, *arrived)
    swap = [(i, i ^ 1) for i in range(dp)]
    got = lax.ppermute(rest, "dp", swap)
    keep, along = call(
        functools.partial(keep_body, steps), [shape((3, chans, chans), F32), shape(chunk, BF16)], [VM] * 5, "keep",
        flops=6 * block * chans, nbytes=20 * block,
    )(mix, xt, ht, act_cot, sums)

    def pairs(p, turn):
        result = []
        for d in range(dp):
            for r in range(regions):
                e, q = (d ^ (2 * p), r) if (d % 2 == 0) == turn else (d, r ^ p)
                result.append((d * regions + r, e * regions + q))
        return result

    def crossed(p, turn):
        return [(i, j ^ regions) for i, j in pairs(p, turn)]

    gots = [lax.ppermute(along, BOTH, pairs(1, True))]
    own, *sends, cross = call(
        split_body, [shape(chunk, F32)] + [shape(chunk, BF16)] * (ways - 1), [VM] * 3, "split"
    )(keep, got, cross)
    gots += [lax.ppermute(part, BOTH, pairs(p, True)) for p, part in list(enumerate(sends, 2))[::-1]]
    gots += [lax.ppermute(cross, BOTH, crossed(1, False))]
    (mine,) = call(sum_body, [shape(chunk, BF16)], [VM] * (ways + 1), "add_first")(own, *gots)
    gots = [lax.ppermute(mine, BOTH, pairs(p, False)) for p in range(1, ways)]
    grad_inputs, token = call(
        functools.partial(inputs_body, steps), [shape(x.shape, BF16), shape((8, 128), F32)], [VM] * 4 + [AN], "inputs",
        flops=8 * block * chans, nbytes=16 * block,
    )(act_cot, cot, w_filter, w_gate, mine)
    (done,) = call(
        functools.partial(add_body, ways), [shape(chunk, BF16)], [VM] * ways + [AN], "add_second"
    )(mine, *gots, token)
    chunks = [done] + [lax.ppermute(done, BOTH, pairs(p, True)) for p in range(1, ways)]
    direct = lax.ppermute(done, BOTH, crossed(1, True))
    others = [direct if i == 1 else lax.ppermute(part, "dp", swap) for i, part in enumerate(chunks)]
    factor = 1.0 / math.sqrt(windows * dp * steps * sites * regions)
    results = [shape((2, chans, chans), F32)] * 3
    extra = dict(out_specs=[HB] * 3, scratch=[pltpu.VMEM((ways,) + chunk, F32), dma((ways, 3))])
    grads = call(functools.partial(scale_body, ways, factor, False), results, [VM] * ways, "scale_own", **extra)(*chunks)
    grads = call(
        functools.partial(scale_body, ways, factor, True), results, [VM] * ways + [HB] * 3, "scale_other",
        aliases={ways + a: a for a in range(3)}, **extra,
    )(*others, *grads)
    return (grad_inputs.reshape(inputs.shape), *grads)


def solution(mesh):
    return jax.shard_map(
        per_device,
        mesh=mesh,
        in_specs=(
            P("dp", None, "region", None),
            P("dp", None, "region", None),
            P(),
            P(),
            P(),
            P(),
            P("region", None, None, None),
        ),
        out_specs=(P("dp", None, "region", None), P(), P(), P()),
        check_vma=False,
    )
```

```python
import functools
import math

import jax
import jax.numpy as jnp
from jax import lax
from jax.experimental import pallas as pl
from jax.experimental.pallas import tpu as pltpu
from jax.sharding import PartitionSpec as P

TILE = 128
F32 = jnp.float32
BF16 = jnp.bfloat16
VM = pl.BlockSpec(memory_space=pltpu.VMEM)
HB = pl.BlockSpec(memory_space=pltpu.HBM)
AN = pl.BlockSpec(memory_space=pl.ANY)
BOTH = ("dp", "region")


def dot(a, b, ca=1, cb=0):
    return lax.dot_general(a, b, (((ca,), (cb,)), ((), ())), preferred_element_type=F32)


def call(body, outs, ins, name, out_specs=None, scratch=(), flops=0, nbytes=0, aliases=None):
    return pl.pallas_call(
        body,
        out_shape=outs,
        in_specs=ins,
        out_specs=out_specs or [VM] * len(outs),
        scratch_shapes=list(scratch),
        cost_estimate=pl.CostEstimate(flops=flops, bytes_accessed=nbytes, transcendentals=0),
        compiler_params=pltpu.CompilerParams(vmem_limit_bytes=40 * 1024 * 1024),
        input_output_aliases=aliases or {},
        name=name,
    )


def in_hbm(*arrays):
    return [pltpu.with_memory_space_constraint(array, pltpu.HBM) for array in arrays]


def fetch(pairs, sems):
    copies = [pltpu.make_async_copy(src, dst, sems.at[i]) for i, (src, dst) in enumerate(pairs)]
    for copy in copies:
        copy.start()
    return copies


def find_entry(nb_ref, source, target, tiles, per_tile):
    tile = jnp.int32(0)
    place = jnp.int32(0)
    named = jnp.int32(-1)
    for j in range(tiles):
        for k in range(per_tile):
            local = nb_ref[source * tiles + j, k] - target * tiles
            hit = jnp.logical_and(local >= 0, local < tiles)
            tile = jnp.where(hit, j, tile)
            place = jnp.where(hit, k, place)
            named = jnp.where(hit, local, named)
    return tile, place, named


def region_of():
    return lax.axis_index("region").astype(jnp.int32)


def lane_of():
    place = lax.axis_index("dp").astype(jnp.int32)
    lane, chip, region = jnp.bitwise_and(place, 1), lax.shift_right_logical(place, 1), region_of()
    return lane, jnp.where(lane == 0, chip, region), jnp.where(lane == 0, region, chip)


def outgoing_body(regions, order, nb_hbm, cot_hbm, adj_hbm, *refs):
    out_refs, (nb_ref, cot_ref, adj_ref, sems) = refs[: regions - 1], refs[regions - 1 :]
    me = region_of()
    tiles, per_tile = adj_ref.shape[:2]
    total = cot_ref.shape[0]
    parts = [(nb_hbm, nb_ref), (cot_hbm, cot_ref), (adj_hbm, adj_ref)]
    first, *copies = fetch(parts, sems)
    first.wait()
    found = [find_entry(nb_ref, me, jnp.bitwise_xor(me, p), tiles, per_tile) for p in order]
    for copy in copies:
        copy.wait()
    for out, (tile, place, _) in zip(out_refs, found):
        weights = adj_ref[tile, place]
        for t in range(total):
            rows = cot_ref[t, pl.ds(pl.multiple_of(tile * TILE, TILE), TILE), :]
            out[t] = dot(weights, rows, 0, 0).astype(BF16)


def local_body(
    steps, order, nb_hbm, x_hbm, cot_hbm, wf_hbm, wg_hbm, wm_hbm, adj_hbm,
    df_ref, dg_ref, direct_ref, local_ref, mix_ref, xt_ref, ht_ref, wt_ref, mask_ref,
    nb_ref, x_ref, cot_ref, wf_ref, wg_ref, wm_ref, adj_ref, sems,
):
    me = region_of()
    tiles, per_tile = adj_ref.shape[:2]
    total = cot_ref.shape[0]
    c_nb, c_x, c_wf, c_wg, c_cot, c_wm, c_adj = fetch(
        [(nb_hbm, nb_ref), (x_hbm, x_ref), (wf_hbm, wf_ref), (wg_hbm, wg_ref), (cot_hbm, cot_ref), (wm_hbm, wm_ref), (adj_hbm, adj_ref)],
        sems,
    )
    c_x.wait()
    c_wf.wait()
    c_wg.wait()
    for t in range(total):
        x = x_ref[t]
        act_f = dot(x, wf_ref[0])
        act_g = dot(x, wg_ref[0])
        if t % steps:
            before = x_ref[t - 1]
            act_f += dot(before, wf_ref[1])
            act_g += dot(before, wg_ref[1])
        filt = jnp.tanh(act_f)
        gate = jax.nn.sigmoid(act_g)
        both = filt * gate
        ht_ref[t] = both.astype(BF16).T
        xt_ref[t] = x.T
        df_ref[t] = gate * (1.0 - filt * filt)
        dg_ref[t] = both * (1.0 - gate)
    c_cot.wait()
    c_wm.wait()
    wt_ref[...] = wm_ref[1].T
    mix = jnp.zeros(mix_ref.shape, F32)
    for t in range(total):
        cot = cot_ref[t]
        direct_ref[t] = dot(cot, wm_ref[0], 1, 1)
        mix += dot(ht_ref[t], cot)
    mix_ref[...] = mix
    local_ref[...] = jnp.zeros_like(local_ref)
    c_nb.wait()
    c_adj.wait()
    for j in range(tiles):
        for k in range(per_tile):
            local = nb_ref[me * tiles + j, k] - me * tiles

            @pl.when(jnp.logical_and(local >= 0, local < tiles))
            def _():
                place = pl.ds(pl.multiple_of(local * TILE, TILE), TILE)
                for t in range(total):
                    local_ref[t, place, :] += dot(adj_ref[j, k], cot_ref[t, j * TILE : (j + 1) * TILE, :], 0, 0)

    for s, p in enumerate(order):
        _, _, named = find_entry(nb_ref, jnp.bitwise_xor(me, p), me, tiles, per_tile)
        for j in range(tiles):
            mask_ref[s, j] = jnp.full(mask_ref.shape[2:], jnp.where(named == j, 1.0, 0.0), F32)


def tap_rows(tap, part, steps, xt_ref, act_ref):
    total = xt_ref.shape[0]
    if tap == 0:
        terms = [dot(xt_ref[t], act_ref[part, t]) for t in range(total)]
    else:
        terms = [dot(xt_ref[t - 1], act_ref[part, t]) for t in range(total) if t % steps]
    return functools.reduce(jnp.add, terms)


def chunk_of(ref, mine, p, rows):
    return ref[:, pl.ds(pl.multiple_of(jnp.bitwise_xor(mine, p) * rows, rows), rows), :]


def swapped(ref):
    return [0, *range(2, ref.shape[0] + 1)]


def half_of(tap, steps, xt_ref, ht_ref, mix_ref, act_ref, sums_ref):
    if tap == 0:
        mix = mix_ref[...]
    else:
        mix = functools.reduce(jnp.add, [dot(ht_ref[t], sums_ref[t]) for t in range(ht_ref.shape[0])])
    return [tap_rows(tap, 0, steps, xt_ref, act_ref), tap_rows(tap, 1, steps, xt_ref, act_ref), mix]


def send_body(regions, steps, df_ref, dg_ref, direct_ref, local_ref, mix_ref, xt_ref, ht_ref, wt_ref, mask_ref, *refs):
    arrived, (act_ref, sums_ref, cross_ref, rest_ref, made_ref) = refs[: regions - 1], refs[regions - 1 :]
    lane, _, other = lane_of()
    total, sites, _ = local_ref.shape
    tiles = sites // TILE
    for t in range(total):
        summed = []
        for j in range(tiles):
            part = local_ref[t, j * TILE : (j + 1) * TILE, :]
            for s in range(regions - 1):
                part += (mask_ref[s, j, :1].astype(BF16) * arrived[s][t]).astype(F32)
            summed.append(part.astype(BF16))
        summed = jnp.concatenate(summed, axis=0)
        sums_ref[t] = summed
        grad = direct_ref[t] + dot(summed, wt_ref[...])
        act_ref[0, t] = (grad * df_ref[t]).astype(BF16)
        act_ref[1, t] = (grad * dg_ref[t]).astype(BF16)
    for tap in range(2):

        @pl.when(lane == 1 - tap)
        def _():
            for i, part in enumerate(half_of(tap, steps, xt_ref, ht_ref, mix_ref, act_ref, sums_ref)):
                made_ref[i] = part

    rows = cross_ref.shape[1]
    cross_ref[...] = chunk_of(made_ref, other, 1, rows).astype(BF16)
    for i, p in enumerate(swapped(rest_ref)):
        rest_ref[i] = chunk_of(made_ref, other, p, rows).astype(BF16)


def keep_body(steps, mix_ref, xt_ref, ht_ref, act_ref, sums_ref, keep_ref, along_ref):
    lane, mine, _ = lane_of()
    for tap in range(2):

        @pl.when(lane == tap)
        def _():
            for i, part in enumerate(half_of(tap, steps, xt_ref, ht_ref, mix_ref, act_ref, sums_ref)):
                keep_ref[i] = part
    along_ref[...] = chunk_of(keep_ref, mine, 1, along_ref.shape[1]).astype(BF16)


def inputs_body(steps, act_ref, cot_ref, wf_ref, wg_ref, _, out_ref, token_ref):
    token_ref[...] = jnp.zeros_like(token_ref)
    total = cot_ref.shape[0]
    for t in range(total):
        grad = cot_ref[t].astype(F32)
        grad += dot(act_ref[0, t], wf_ref[0], 1, 1) + dot(act_ref[1, t], wg_ref[0], 1, 1)
        if (t + 1) % steps:
            grad += dot(act_ref[0, t + 1], wf_ref[1], 1, 1) + dot(act_ref[1, t + 1], wg_ref[1], 1, 1)
        out_ref[t] = grad.astype(BF16)


def split_body(keep_ref, got_ref, cross_ref, own_ref, *sends):
    _, mine, _ = lane_of()
    sends[-1][...] = cross_ref[...]
    for i, p in enumerate(swapped(got_ref)):
        part = chunk_of(keep_ref, mine, p, own_ref.shape[1]) + got_ref[i].astype(F32)
        if i == 0:
            own_ref[...] = part
        else:
            sends[i - 1][...] = part.astype(BF16)


def tree(parts):
    while len(parts) > 1:
        parts = [parts[i] + parts[i + 1] for i in range(0, len(parts), 2)]
    return parts[0]


def sum_body(*refs):
    refs[-1][...] = functools.reduce(jnp.add, [ref[...].astype(F32) for ref in refs[:-1]]).astype(BF16)


def add_body(ways, *refs):
    refs[-1][...] = tree([ref[...].astype(F32) for ref in refs[:ways]]).astype(BF16)


def scale_body(ways, factor, other, *refs):
    chunks, refs = refs[:ways], refs[ways:]
    outs, (held, sems) = refs[-5:-2], refs[-2:]
    lane, first, second = lane_of()
    tap, mine = (1 - lane, second) if other else (lane, first)
    rows = chunks[0].shape[1]
    copies = []
    for p in range(ways):
        place = pl.ds(pl.multiple_of(jnp.bitwise_xor(mine, p) * rows, rows), rows)
        for a in range(3):
            held[p, a] = chunks[p][a].astype(F32) * factor
            copy = pltpu.make_async_copy(held.at[p, a], outs[a].at[tap, place], sems.at[p, a])
            copy.start()
            copies.append(copy)
    for copy in copies:
        copy.wait()


def per_device(inputs, cotangent, w_filter, w_gate, w_mix, neighbours, adjacency):
    regions = lax.axis_size("region")
    dp = lax.axis_size("dp")
    ways = dp // 2
    assert ways == regions
    windows, steps, sites, chans = inputs.shape
    total = windows * steps
    tiles, per_tile = adjacency.shape[:2]
    x = inputs.reshape(total, sites, chans)
    cot = cotangent.reshape(total, sites, chans)
    shape = jax.ShapeDtypeStruct
    block = total * sites * chans
    order = sorted(range(1, regions), key=lambda p: p != regions // 2)
    dma = pltpu.SemaphoreType.DMA

    outgoing = call(
        functools.partial(outgoing_body, regions, order),
        [shape((total, TILE, chans), BF16)] * (regions - 1), [HB] * 3, "outgoing",
        scratch=[
            pltpu.SMEM(neighbours.shape, jnp.int32), pltpu.VMEM(cot.shape, BF16), pltpu.VMEM(adjacency.shape, BF16),
            dma((3,)),
        ],
        flops=2 * (regions - 1) * total * TILE * TILE * chans, nbytes=4 * block,
    )(*in_hbm(neighbours, cot, adjacency))
    arrived = [
        lax.ppermute(part, "region", [(r, r ^ p) for r in range(regions)]) for p, part in zip(order, outgoing)
    ]
    square = shape((chans, chans), F32)
    turned = shape((total, chans, sites), BF16)
    d_filter, d_gate, direct, local, mix, xt, ht, wt, mask = call(
        functools.partial(local_body, steps, order),
        [shape(x.shape, F32)] * 4
        + [square, turned, turned, shape((chans, chans), BF16), shape((regions - 1, tiles, 8, chans), F32)],
        [HB] * 7, "local",
        scratch=[
            pltpu.SMEM(neighbours.shape, jnp.int32), pltpu.VMEM(x.shape, BF16), pltpu.VMEM(x.shape, BF16),
            pltpu.VMEM(w_filter.shape, BF16), pltpu.VMEM(w_gate.shape, BF16), pltpu.VMEM(w_mix.shape, BF16),
            pltpu.VMEM(adjacency.shape, BF16), dma((7,)),
        ],
        flops=14 * block * chans, nbytes=30 * block,
    )(*in_hbm(neighbours, x, cot, w_filter, w_gate, w_mix, adjacency))
    rows = chans // ways
    chunk = (3, rows, chans)
    act_cot, sums, cross, rest = call(
        functools.partial(send_body, regions, steps),
        [shape((2,) + x.shape, BF16), shape(x.shape, BF16), shape(chunk, BF16), shape((ways - 1,) + chunk, BF16)],
        [VM] * (9 + regions - 1), "send", scratch=[pltpu.VMEM((3, chans, chans), F32)],
        flops=6 * block * chans, nbytes=30 * block,
    )(d_filter, d_gate, direct, local, mix, xt, ht, wt, mask, *arrived)
    swap = [(i, i ^ 1) for i in range(dp)]
    got = lax.ppermute(rest, "dp", swap)
    keep, along = call(
        functools.partial(keep_body, steps), [shape((3, chans, chans), F32), shape(chunk, BF16)], [VM] * 5, "keep",
        flops=6 * block * chans, nbytes=20 * block,
    )(mix, xt, ht, act_cot, sums)

    def pairs(p, turn):
        result = []
        for d in range(dp):
            for r in range(regions):
                e, q = (d ^ (2 * p), r) if (d % 2 == 0) == turn else (d, r ^ p)
                result.append((d * regions + r, e * regions + q))
        return result

    def crossed(p, turn):
        return [(i, j ^ regions) for i, j in pairs(p, turn)]

    gots = [lax.ppermute(along, BOTH, pairs(1, True))]
    own, *sends, cross = call(
        split_body, [shape(chunk, F32)] + [shape(chunk, BF16)] * (ways - 1), [VM] * 3, "split"
    )(keep, got, cross)
    gots += [lax.ppermute(part, BOTH, pairs(p, True)) for p, part in list(enumerate(sends, 2))[::-1]]
    gots += [lax.ppermute(cross, BOTH, crossed(1, False))]
    (mine,) = call(sum_body, [shape(chunk, BF16)], [VM] * (ways + 1), "add_first")(own, *gots)
    gots = [lax.ppermute(mine, BOTH, pairs(p, False)) for p in range(1, ways)[::-1]][::-1]
    grad_inputs, token = call(
        functools.partial(inputs_body, steps), [shape(x.shape, BF16), shape((8, 128), F32)], [VM] * 4 + [AN], "inputs",
        flops=8 * block * chans, nbytes=16 * block,
    )(act_cot, cot, w_filter, w_gate, mine)
    (done,) = call(
        functools.partial(add_body, ways), [shape(chunk, BF16)], [VM] * ways + [AN], "add_second"
    )(mine, *gots, token)
    near = {p: lax.ppermute(done, BOTH, pairs(p, True)) for p in [*range(2, ways), 1][::-1]}
    chunks = [done] + [near[p] for p in range(1, ways)]
    direct = lax.ppermute(done, BOTH, crossed(1, True))
    others = [direct if i == 1 else lax.ppermute(part, "dp", swap) for i, part in enumerate(chunks)]
    factor = 1.0 / math.sqrt(windows * dp * steps * sites * regions)
    results = [shape((2, chans, chans), F32)] * 3
    extra = dict(out_specs=[HB] * 3, scratch=[pltpu.VMEM((ways,) + chunk, F32), dma((ways, 3))])
    grads = call(functools.partial(scale_body, ways, factor, False), results, [VM] * ways, "scale_own", **extra)(*chunks)
    grads = call(
        functools.partial(scale_body, ways, factor, True), results, [VM] * ways + [HB] * 3, "scale_other",
        aliases={ways + a: a for a in range(3)}, **extra,
    )(*others, *grads)
    return (grad_inputs.reshape(inputs.shape), *grads)


def solution(mesh):
    return jax.shard_map(
        per_device,
        mesh=mesh,
        in_specs=(
            P("dp", None, "region", None),
            P("dp", None, "region", None),
            P(),
            P(),
            P(),
            P(),
            P("region", None, None, None),
        ),
        out_specs=(P("dp", None, "region", None), P(), P(), P()),
        check_vma=False,
    )
```
